256 devices in a mesh: group: 2 (over z_lo), dp: 32 (over x, z_hi, core), mp: 4 (over y).
Axes of the slice: x: 4, y: 4, z: 8 (z_hi: 4, z_lo: 2; z = z_hi * 2 + z_lo), core: 2. Of those that a mesh axis runs over, the one named last changes fastest.
Arguments:
- states: bfloat16 [4096, 4096], P('dp', 'mp'), may hold values from -18 to 18
- neighbours: bfloat16 [128, 64, 4096], P('dp', None, 'mp'), may hold values from -18 to 18
- cotangent: bfloat16 [4096, 4096], P('dp', 'mp'), may hold values from -24 to 24
- span_of: int32 [128], P('dp'), may hold values from 0 to 63, as said below
- counts: int32 [32], P('dp'), may hold values from 2 to 4, as said below
- kv_weight: bfloat16 [2, 4096, 2, 4096], P('group', 'dp', None, 'mp'), may hold values from -1 to 1
- gains: float32 [2, 2, 4096], P('group', None, 'mp'), may hold values from 0.5 to 3
Outputs:
- results: float32 [2, 4096, 4096], P('group', 'dp', 'mp')
The draws below stay inside these ranges and needn't reach their ends.
Inputs may be any that keep to these rules, and one draw needn't show every extreme that they name: `span_of`: slot j of dp shard d (row d * 4 + j) names a span of the same shard, d * 2 to d * 2 + 1. The live slots of a shard name its spans in order, every span by one or two slots. `counts`: the live slots of a shard lead its slots; some shard has all 4 live.
All inputs are finite; a program needn't handle non-finite values.
Results may differ from the reference program's by a relative error of at most 0.029.
Values may be sent and summed in bfloat16 or wider, within the bound.
A program may use at most 128 MiB of HBM per device.

```python
import math
import jax
import jax.numpy as jnp
from jax import lax

HEADS = 32
HD = 128
HEAD_FEATURES = 4096
CH = 64
NEIGHBOUR_TOKENS = 64
SPAN_DEV = 2
SLOTS = 4
TOKENS = 4096
NEIGHBOUR_SLOTS = 128
N_DP = 32


def neighbour_layout(key):
    key_counts, key_full, key_spare = jax.random.split(key, 3)
    per_span = jax.random.randint(key_counts, (N_DP, SPAN_DEV), 1, 3)
    full_shard = jax.random.randint(key_full, (), 0, N_DP)
    per_span = jnp.where((jnp.arange(N_DP) == full_shard)[:, None], 2, per_span)
    span_ends = jnp.cumsum(per_span, axis=1)
    active_row_counts = span_ends[:, -1]
    slot_index = jnp.arange(SLOTS)
    local_span = jnp.sum((span_ends[:, None, :] <= slot_index[None, :, None]).astype(jnp.int32), axis=2)
    spare_span = jax.random.randint(key_spare, (N_DP, SLOTS), 0, SPAN_DEV)
    local_span = jnp.where(slot_index[None, :] < active_row_counts[:, None], local_span, spare_span)
    span_index_list = local_span + jnp.arange(N_DP)[:, None] * SPAN_DEV
    return (span_index_list.reshape(NEIGHBOUR_SLOTS).astype(jnp.int32), active_row_counts.astype(jnp.int32))


def draw_span_of(key, part):
    span_index_list, active_row_counts = neighbour_layout(key)
    return span_index_list


def draw_counts(key, part):
    span_index_list, active_row_counts = neighbour_layout(key)
    return active_row_counts


def draw_states(key, part):
    key = jax.random.fold_in(key, 21)
    input_rows = jax.random.truncated_normal(key, -6.0, 6.0, (TOKENS, HEAD_FEATURES), jnp.float32)
    return input_rows.astype(jnp.bfloat16)


def draw_neighbours(key, part):
    key = jax.random.fold_in(key, 22)
    key_row_block = jax.random.fold_in(key, 0)
    input_rows = jax.random.truncated_normal(key_row_block, -6.0, 6.0, (NEIGHBOUR_SLOTS, NEIGHBOUR_TOKENS, HEAD_FEATURES), jnp.float32)
    return input_rows.astype(jnp.bfloat16)


def draw_kv_weight(key, part):
    key = jax.random.fold_in(key, 23)
    weights = jax.random.truncated_normal(key, -6.0, 6.0, (2, HEAD_FEATURES, 2, HEAD_FEATURES), jnp.float32) * HEAD_FEATURES ** (-0.5)
    return weights.astype(jnp.bfloat16)


def shard_levels(own_key, dims, pieces, least, largest):
    gain, own = 1.0, jax.random.fold_in(own_key, 6)
    for axis_at, shards_of in pieces:
        draws = jnp.exp(jax.random.uniform(jax.random.fold_in(own, axis_at), (shards_of,), jnp.float32, least / len(pieces), largest / len(pieces)))
        gain = gain * jnp.repeat(draws, dims[axis_at] // shards_of).reshape([-1 if axis == axis_at else 1 for axis in range(len(dims))])
    return gain


def noise(rng, dims, width, reach, cuts=(), held_as=jnp.bfloat16):
    array = jax.random.normal(rng, dims, jnp.float32) * width
    if len(cuts) > 0:
        array = shard_levels(rng, dims, cuts, -0.22, 0.18) * array
    return jnp.clip(array, min=-reach, max=reach).astype(held_as)


def setup_inputs(seed: int = 0) -> dict:
    splits = jax.random.split(jax.random.key(seed), 8)
    return {
        "states": draw_states(jax.random.fold_in(splits[7], 71), 0),
        "neighbours": draw_neighbours(jax.random.fold_in(splits[7], 71), 0),
        "cotangent": noise(splits[2], (TOKENS, HEAD_FEATURES), 4.0, 24.0, ((0, 32), (1, 4))),
        "span_of": draw_span_of(jax.random.fold_in(splits[7], 71), 0),
        "counts": draw_counts(jax.random.fold_in(splits[7], 71), 0),
        "kv_weight": draw_kv_weight(jax.random.fold_in(splits[7], 71), 0),
        "gains": jnp.clip(jnp.exp(math.log(3.0) - 1.7917595 * jax.random.uniform(splits[6], (2, 2, HEAD_FEATURES), jnp.float32) ** shard_levels(splits[6], (2, 2, HEAD_FEATURES), ((0, 2), (2, 4)), -0.2, 0.2)), 0.5, 3.0),
    }


EPSILON = 1e-05
NEG_LARGE = -1e+30

def settle(values):
    return lax.optimization_barrier(values.astype(jnp.bfloat16)).astype(jnp.float32)

def masked_softmax(scores, key_mask):
    masked_scores = jnp.where(key_mask, scores, NEG_LARGE)
    highest = lax.optimization_barrier(jnp.max(masked_scores, axis=-1, keepdims=True))
    raised = jnp.where(key_mask, jnp.exp(masked_scores - highest), 0.0)
    return raised / lax.optimization_barrier(jnp.sum(raised, axis=-1, keepdims=True))

def weights_of(queries, key_heads, key_mask):
    scores = jnp.einsum('qhd,khd->hqk', queries, key_heads) * HD ** (-0.5)
    attn_probs = masked_softmax(scores, key_mask[None])
    return (attn_probs, settle(attn_probs))

def attend_back(grad_out, queries, values, attn_probs, rounded):
    grad_values = jnp.einsum('hqk,qhd->khd', rounded, grad_out)
    grad_probs = jnp.einsum('qhd,khd->hqk', grad_out, values)
    grad_scores = attn_probs * (grad_probs - lax.optimization_barrier(jnp.sum(grad_probs * attn_probs, axis=-1, keepdims=True)))
    grad_keys = HD ** (-0.5) * jnp.einsum('hqk,qhd->khd', grad_scores, queries)
    return (grad_keys, grad_values)

def inverse_rms(rows_f):
    return lax.rsqrt(lax.optimization_barrier(jnp.mean(rows_f * rows_f, axis=1)) + EPSILON)

def reference(states, neighbours, cotangent, span_of, counts, kv_weight, gains):
    tok_rows = CH * SPAN_DEV
    row_count = SLOTS * NEIGHBOUR_TOKENS
    state_f = states.astype(jnp.float32)
    inv_state = inverse_rms(state_f)
    dec_queries = settle(state_f * inv_state[:, None] * gains[0, 0])
    state_input = (state_f * inv_state[:, None] * gains[1, 0]).astype(jnp.bfloat16)
    decoder_weight = kv_weight[0].reshape(HEAD_FEATURES, 2 * HEAD_FEATURES)
    weight_enc = kv_weight[1].reshape(HEAD_FEATURES, 2 * HEAD_FEATURES)
    state_kv = jnp.dot(state_input, weight_enc, preferred_element_type=jnp.float32).astype(jnp.bfloat16)
    state_kv = state_kv.reshape(TOKENS, 2, HEAD_FEATURES)
    neighbour_float_rows = neighbours.reshape(NEIGHBOUR_SLOTS * NEIGHBOUR_TOKENS, HEAD_FEATURES).astype(jnp.float32)
    inv_neigh = inverse_rms(neighbour_float_rows)
    enc_queries = settle(neighbour_float_rows * inv_neigh[:, None] * gains[1, 1])
    token_span = jnp.arange(tok_rows, dtype=jnp.int32) // CH
    slot_index = jnp.arange(SLOTS, dtype=jnp.int32)
    shard_index_list = jnp.arange(N_DP, dtype=jnp.int32)

    def shard_masks(shard_id):
        local_span = lax.dynamic_slice_in_dim(span_of, shard_id * SLOTS, SLOTS) - shard_id * SPAN_DEV
        row_span = jnp.repeat(local_span, NEIGHBOUR_TOKENS)
        live_rows = jnp.repeat(slot_index < counts[shard_id], NEIGHBOUR_TOKENS)
        return (row_span, live_rows)

    def shard_state_kv(shard_id):
        kv_pair = lax.dynamic_slice_in_dim(state_kv, shard_id * tok_rows, tok_rows).astype(jnp.float32)
        return (kv_pair[:, 0].reshape(tok_rows, HEADS, HD), kv_pair[:, 1].reshape(tok_rows, HEADS, HD))

    def encoder_shard_pass(shard_id):
        row_span, live_rows = shard_masks(shard_id)
        queries = lax.dynamic_slice_in_dim(enc_queries, shard_id * row_count, row_count).reshape(row_count, HEADS, HD)
        key_heads, values = shard_state_kv(shard_id)
        key_mask = row_span[:, None] == token_span[None, :]
        attn_probs, rounded = weights_of(queries, key_heads, key_mask)
        output = jnp.einsum('hqk,khd->qhd', rounded, values)
        residual = lax.dynamic_slice_in_dim(neighbour_float_rows, shard_id * row_count, row_count)
        return (residual + output.reshape(row_count, HEAD_FEATURES)).astype(jnp.bfloat16)
    encoder_output = lax.map(encoder_shard_pass, shard_index_list).reshape(NEIGHBOUR_SLOTS * NEIGHBOUR_TOKENS, HEAD_FEATURES)
    enc_f = encoder_output.astype(jnp.float32)
    inv_enc = inverse_rms(enc_f)
    enc_input = (enc_f * inv_enc[:, None] * gains[0, 1]).astype(jnp.bfloat16)
    neighbour_key_value = jnp.dot(enc_input, decoder_weight, preferred_element_type=jnp.float32).astype(jnp.bfloat16)
    neighbour_key_value = neighbour_key_value.reshape(NEIGHBOUR_SLOTS * NEIGHBOUR_TOKENS, 2, HEAD_FEATURES)
    cot_f = cotangent.astype(jnp.float32)

    def decode_shard(shard_id):
        row_span, live_rows = shard_masks(shard_id)
        queries = lax.dynamic_slice_in_dim(dec_queries, shard_id * tok_rows, tok_rows).reshape(tok_rows, HEADS, HD)
        kv_pair = lax.dynamic_slice_in_dim(neighbour_key_value, shard_id * row_count, row_count).astype(jnp.float32)
        key_heads = kv_pair[:, 0].reshape(row_count, HEADS, HD)
        values = kv_pair[:, 1].reshape(row_count, HEADS, HD)
        key_mask = (token_span[:, None] == row_span[None, :]) & live_rows[None, :]
        attn_probs, rounded = weights_of(queries, key_heads, key_mask)
        output = jnp.einsum('hqk,khd->qhd', rounded, values)
        mixed_rows = lax.dynamic_slice_in_dim(state_f, shard_id * tok_rows, tok_rows) + output.reshape(tok_rows, HEAD_FEATURES)
        grad_out = lax.dynamic_slice_in_dim(cot_f, shard_id * tok_rows, tok_rows).reshape(tok_rows, HEADS, HD)
        grad_keys, grad_values = attend_back(grad_out, queries, values, attn_probs, rounded)
        grad_pair = jnp.stack([grad_keys.reshape(row_count, HEAD_FEATURES), grad_values.reshape(row_count, HEAD_FEATURES)], axis=1)
        return (mixed_rows, grad_pair.astype(jnp.bfloat16))
    mixed, neighbour_kv_gradient = lax.map(decode_shard, shard_index_list)
    mixed = mixed.reshape(TOKENS, HEAD_FEATURES)
    encoder_input_gradient = jnp.dot(neighbour_kv_gradient.reshape(NEIGHBOUR_SLOTS * NEIGHBOUR_TOKENS, 2 * HEAD_FEATURES), decoder_weight.T, preferred_element_type=jnp.float32)
    enc_dot = lax.optimization_barrier(jnp.sum(gains[0, 1] * enc_f * encoder_input_gradient, axis=1))
    grad_encoded = settle(inv_enc[:, None] * gains[0, 1] * encoder_input_gradient - enc_f * (inv_enc ** 3 * enc_dot / HEAD_FEATURES)[:, None])

    def back_shard(shard_id):
        row_span, live_rows = shard_masks(shard_id)
        queries = lax.dynamic_slice_in_dim(enc_queries, shard_id * row_count, row_count).reshape(row_count, HEADS, HD)
        key_heads, values = shard_state_kv(shard_id)
        key_mask = row_span[:, None] == token_span[None, :]
        attn_probs, rounded = weights_of(queries, key_heads, key_mask)
        grad_out = lax.dynamic_slice_in_dim(grad_encoded, shard_id * row_count, row_count).reshape(row_count, HEADS, HD)
        grad_keys, grad_values = attend_back(grad_out, queries, values, attn_probs, rounded)
        grad_pair = jnp.stack([grad_keys.reshape(tok_rows, HEAD_FEATURES), grad_values.reshape(tok_rows, HEAD_FEATURES)], axis=1)
        return grad_pair.astype(jnp.bfloat16)
    grad_state_kv = lax.map(back_shard, shard_index_list).reshape(TOKENS, 2 * HEAD_FEATURES)
    grad_state_input = jnp.dot(grad_state_kv, weight_enc.T, preferred_element_type=jnp.float32)
    state_dot = lax.optimization_barrier(jnp.sum(gains[1, 0] * state_f * grad_state_input, axis=1))
    grad_states = inv_state[:, None] * gains[1, 0] * grad_state_input - state_f * (inv_state ** 3 * state_dot / HEAD_FEATURES)[:, None]
    return jnp.stack([mixed, grad_states])
```

```python
import functools

import jax
import jax.numpy as jnp
from jax import lax
from jax.experimental import pallas as pl
from jax.experimental.pallas import tpu as pltpu
from jax.sharding import PartitionSpec as P

HD = 128
FEATURES = 4096
CH = 64
EPSILON = 1e-05
NEG_LARGE = -1e30
TOK = 128
ROWS = 256
COLS = 1024
HALF = 512
HEADS = 4
SCALE = HD ** (-0.5)
BF = jnp.bfloat16
F32 = jnp.float32
SEMS = 224


def nt(a, b):
    return lax.dot_general(a, b, (((1,), (1,)), ((), ())), preferred_element_type=F32)


def nn(a, b):
    return lax.dot_general(a, b, (((1,), (0,)), ((), ())), preferred_element_type=F32)


def tn(a, b):
    return lax.dot_general(a, b, (((0,), (0,)), ((), ())), preferred_element_type=F32)


class Comm:
    def __init__(self, ssem, rsem):
        self.ssem, self.rsem = ssem, rsem
        self.used, self.sent = 0, []

    def alloc(self, count):
        base = self.used
        self.used += count
        assert self.used <= SEMS
        return base

    def copy(self, slot, src, dst, dev):
        return pltpu.make_async_remote_copy(
            src_ref=src,
            dst_ref=dst,
            send_sem=self.ssem.at[slot],
            recv_sem=self.rsem.at[slot],
            device_id=dev,
            device_id_type=pl.DeviceIdType.MESH,
        )

    def send(self, slot, src, dst, dev):
        copy = self.copy(slot, src, dst, dev)
        copy.start()
        self.sent.append(copy)

    def recv(self, slot, dst, dev):
        self.copy(slot, dst, dst, dev).wait_recv()

    def drain(self):
        for copy in self.sent:
            copy.wait_send()


class Ring:
    def __init__(self, comm, half, plus, minus):
        self.comm, self.half, self.plus, self.minus = comm, half, plus, minus
        self.base = comm.alloc(6)

    def start(self):
        for slot, k, dev in ((0, 0, self.plus), (2, 1, self.minus), (1, 1, self.plus), (3, 0, self.minus)):
            self.comm.send(self.base + slot, self.half(0, k), self.half(0, k), dev)

    def forward(self):
        self.comm.recv(self.base, self.half(-1, 0), self.minus)
        self.comm.send(self.base + 4, self.half(-1, 0), self.half(-1, 0), self.plus)
        self.comm.recv(self.base + 2, self.half(1, 1), self.plus)
        self.comm.send(self.base + 5, self.half(1, 1), self.half(1, 1), self.minus)

    def near(self):
        self.comm.recv(self.base + 1, self.half(-1, 1), self.minus)
        self.comm.recv(self.base + 3, self.half(1, 0), self.plus)

    def far(self):
        self.comm.recv(self.base + 4, self.half(2, 0), self.minus)
        self.comm.recv(self.base + 5, self.half(2, 1), self.plus)


class Scatter:
    def __init__(self, comm, part, bufs, plus, minus, rows):
        self.comm, self.part, self.plus, self.minus, self.n = comm, part, plus, minus, rows // 2
        self.from_minus, self.from_plus, self.last_minus, self.last_plus = bufs
        self.base = comm.alloc(6)

    def lo(self, ref):
        return ref.at[pl.ds(0, self.n), :]

    def hi(self, ref):
        return ref.at[pl.ds(self.n, self.n), :]

    def first(self):
        self.comm.send(self.base, self.lo(self.part(2)), self.from_minus, self.plus)
        self.comm.send(self.base + 1, self.hi(self.part(2)), self.from_plus, self.minus)

    def second(self):
        self.comm.send(self.base + 2, self.hi(self.part(1)), self.hi(self.last_minus), self.plus)
        self.comm.send(self.base + 3, self.lo(self.part(-1)), self.lo(self.last_plus), self.minus)

    def third(self):
        self.comm.recv(self.base, self.from_minus, self.minus)
        a = self.lo(self.part(1))
        a[...] = (a[...].astype(F32) + self.from_minus[...].astype(F32)).astype(BF)
        self.comm.send(self.base + 4, a, self.lo(self.last_minus), self.plus)
        self.comm.recv(self.base + 1, self.from_plus, self.plus)
        b = self.hi(self.part(-1))
        b[...] = (b[...].astype(F32) + self.from_plus[...].astype(F32)).astype(BF)
        self.comm.send(self.base + 5, b, self.hi(self.last_plus), self.minus)

    def total(self):
        self.comm.recv(self.base + 2, self.hi(self.last_minus), self.minus)
        self.comm.recv(self.base + 3, self.lo(self.last_plus), self.plus)
        self.comm.recv(self.base + 4, self.lo(self.last_minus), self.minus)
        self.comm.recv(self.base + 5, self.hi(self.last_plus), self.plus)
        return (
            self.part(0)[...].astype(F32)
            + self.last_minus[...].astype(F32)
            + self.last_plus[...].astype(F32)
        )


def as_row(col):
    return jnp.transpose(jnp.broadcast_to(col, (col.shape[0], 128)))[0:8, :]


def as_col(row):
    return jnp.transpose(jnp.broadcast_to(row[0:1, :], (128, row.shape[1])))[:, 0:1]


def kernel(
    wsrc, states, neigh, cot, span, counts, gains, out,
    w1, w0, sx, xn, gb, ns, eb, en, acc1, skv, qe, pe, acc2, nkv, dq, g2, pb, rba, rbb, r3, ysum,
    g1, pb1, rca, rcb, t3, ysum1, rd, rdp, rd1, rdp1, mxs, mxr,
    ssem, rsem, lsem,
):
    g = lax.axis_index("group")
    d = lax.axis_index("dp")
    y = lax.axis_index("mp")
    x, zh, c = d // 8, (d // 2) % 4, d % 2
    comm = Comm(ssem, rsem)

    def mod4(v):
        return (v + 4) % 4

    def at_x(r):
        return {"dp": mod4(x + r) * 8 + zh * 2 + c}

    def at_z(r):
        return {"dp": x * 8 + mod4(zh + r) * 2 + c}

    def at_y(r):
        return {"mp": mod4(y + r)}

    partner = {"group": 1 - g}
    sibling = {"dp": d + 1 - 2 * c}
    xp, xm, zp, zm, yp, ym, y2 = at_x(1), at_x(-1), at_z(1), at_z(-1), at_y(1), at_y(-1), at_y(2)

    barrier = pltpu.get_barrier_semaphore()
    peers = (partner, sibling, xp, xm, zp, zm, yp, ym, y2)
    for dev in peers:
        pl.semaphore_signal(barrier, inc=1, device_id=dev, device_id_type=pl.DeviceIdType.MESH)
    pl.semaphore_wait(barrier, len(peers))

    def wrow(rx, rz, core):
        return pl.multiple_of((mod4(x + rx) * 8 + mod4(zh + rz) * 2 + core) * TOK, TOK)

    own_rows = pl.ds(wrow(0, 0, c), TOK)

    def exchange(w, owner):
        local = pltpu.make_async_copy(wsrc.at[g], w.at[own_rows, :], lsem.at[owner])
        away = comm.copy(comm.alloc(1), wsrc.at[1 - g], w.at[own_rows, :], partner)

        @pl.when(g == owner)
        def _():
            away.start()
            local.start()

        def ready():
            @pl.when(g == owner)
            def _():
                local.wait()

            @pl.when(g != owner)
            def _():
                away.wait_recv()

        def done():
            @pl.when(g == owner)
            def _():
                away.wait_send()

        return ready, done

    ready1, done1 = exchange(w1, 1)
    ready0, done0 = exchange(w0, 0)

    def gather(w, ready, state):
        def block(rx, rz, core):
            return w.at[pl.ds(wrow(rx, rz, core), TOK), :]

        def half(rx, rz, k):
            return w.at[pl.ds(pl.multiple_of(wrow(rx, rz, c) + k * 64, 64), 64), :]

        sib_base = comm.alloc(16)

        def sib(rx, rz):
            comm.send(sib_base + (rx % 4) * 4 + rz % 4, block(rx, rz, c), block(rx, rz, c), sibling)

        def sib_wait(rz):
            for rx in range(4):
                comm.recv(sib_base + rx * 4 + rz % 4, block(rx, rz, 1 - c), sibling)

        state["wait"] = sib_wait
        zr = Ring(comm, lambda r, k: half(0, r, k), zp, zm)
        xr = {
            rz: Ring(comm, functools.partial(lambda rz, r, k: half(r, rz, k), rz), xp, xm)
            for rz in (0, -1, 1, 2)
        }
        ready()
        zr.start()
        yield
        xr[0].start()
        sib(0, 0)
        yield
        zr.forward()
        xr[0].forward()
        yield
        zr.near()
        for rz in (-1, 1):
            xr[rz].start()
            sib(0, rz)
        yield
        xr[0].near()
        sib(-1, 0)
        sib(1, 0)
        xr[0].far()
        sib(2, 0)
        yield
        zr.far()
        xr[2].start()
        sib(0, 2)
        yield
        xr[-1].forward()
        xr[1].forward()
        yield
        for rz in (-1, 1):
            xr[rz].near()
            sib(-1, rz)
            sib(1, rz)
        xr[2].forward()
        yield
        for rz in (-1, 1):
            xr[rz].far()
            sib(2, rz)
        yield
        xr[2].near()
        sib(-1, 2)
        sib(1, 2)
        xr[2].far()
        sib(2, 2)
        yield

    st1, st0 = {}, {}
    run1, run0 = gather(w1, ready1, st1), gather(w0, ready0, st0)

    def shalf(r, k):
        return sx.at[mod4(y + r), pl.ds(k * 64, 64), :]

    sx[y] = states[...]
    even = lax.broadcasted_iota(jnp.int32, (8, COLS), 0) % 2 == 0
    gb[y, g] = jnp.where(even, gains[0:1, :], gains[1:2, :])
    sring = Ring(comm, shalf, yp, ym)
    sring.start()
    gain_slot = comm.alloc(4)
    comm.send(gain_slot, gb.at[y, g], gb.at[y, g], partner)
    next(run1)
    next(run1)

    def small_start(buf, base):
        for i, (r, dev) in enumerate(((1, yp), (-1, ym), (2, y2))):
            comm.send(base + i, buf.at[y], buf.at[y], dev)

    def small_wait(buf, base):
        for i, (r, dev) in enumerate(((-1, ym), (1, yp), (2, y2))):
            comm.recv(base + i, buf.at[mod4(y + r)], dev)

    nf = neigh[...].astype(F32)
    ns[y] = as_row(jnp.sum(nf * nf, axis=1, keepdims=True))
    ns_base = comm.alloc(3)
    small_start(ns, ns_base)
    comm.recv(gain_slot, gb.at[y, 1 - g], partner)
    small_start(gb, gain_slot + 1)
    sring.forward()
    next(run1)
    sring.near()
    sring.far()
    small_wait(ns, ns_base)
    small_wait(gb, gain_slot + 1)

    mine = pl.ds(pl.multiple_of(g * HALF, HALF), HALF)
    sums = jnp.zeros((TOK, 1), F32)
    for i in range(4):
        v = sx[i].astype(F32)
        sums = sums + jnp.sum(v * v, axis=1, keepdims=True)
    inv_state = lax.rsqrt(sums / FEATURES + EPSILON)

    def norm_states(i, carry):
        xn[i] = (sx[i].astype(F32) * inv_state * gb[i, 1, 0:1, :]).astype(BF)
        return carry

    lax.fori_loop(0, 4, norm_states, 0)
    dq[...] = (states[:, mine].astype(F32) * inv_state * gb[y, 0, 0:1, mine]).astype(BF)
    inv_neigh = as_col(lax.rsqrt((ns[0] + ns[1] + ns[2] + ns[3]) / FEATURES + EPSILON))
    qe[...] = (neigh[:, mine].astype(F32) * inv_neigh * gb[y, 1, 1:2, mine]).astype(BF)

    def project_states(rz, first):
        st1["wait"](rz)
        z = mod4(zh + rz)

        def step(i, carry):
            rows = pl.ds(pl.multiple_of((i * 4 + z) * 256, 256), 256)
            part = nn(xn[i, :, pl.ds(pl.multiple_of(z * 256, 256), 256)], w1[rows, :])
            acc1[...] += part
            return carry

        if first:
            acc1[...] = jnp.zeros_like(acc1)
        lax.fori_loop(0, 4, step, 0)

    next(run1)
    next(run1)
    next(run1)
    next(run0)
    project_states(0, True)
    next(run1)
    next(run1)
    next(run1)
    next(run0)
    project_states(-1, False)
    project_states(1, False)
    next(run1)
    project_states(2, False)
    skv[...] = acc1[...].astype(BF)

    base_span = d * 2

    def spans_of(slot):
        spans = [span[i] - base_span for i in range(4)]
        return jnp.where(
            slot == 0, spans[0], jnp.where(slot == 1, spans[1], jnp.where(slot == 2, spans[2], spans[3]))
        )

    def iota(shape, axis):
        return lax.broadcasted_iota(jnp.int32, shape, axis)

    enc_mask = spans_of(iota((ROWS, TOK), 0) >> 6) == (iota((ROWS, TOK), 1) >> 6)
    slots_t = iota((TOK, ROWS), 1) >> 6
    dec_mask = (spans_of(slots_t) == (iota((TOK, ROWS), 0) >> 6)) & (slots_t < counts[0])

    def softmax(scores, mask):
        scores = jnp.where(mask, scores * SCALE, NEG_LARGE)
        top = jnp.max(scores, axis=-1, keepdims=True)
        raised = jnp.where(mask, jnp.exp(scores - top), 0.0)
        return raised / jnp.sum(raised, axis=-1, keepdims=True)

    def head(i, second=False):
        start = i * HD + (HALF if second else 0)
        return slice(start, start + HD)

    def mine_head(i):
        return pl.ds(pl.multiple_of(g * HALF + i * HD, HD), HD)

    me8 = y * 2 + g
    for i in range(HEADS):
        probs = softmax(nt(qe[:, head(i)], skv[:, head(i)]), enc_mask)
        pe[i] = probs
        o = nn(probs.astype(BF), skv[:, head(i, True)])
        eb[me8, :, head(i)] = (neigh[:, mine_head(i)].astype(F32) + o).astype(BF)

    def ehalf(grp):
        return lambda r, k: eb.at[mod4(y + r) * 2 + grp, pl.ds(k * 128, 128), :]

    e_slot = comm.alloc(1)
    comm.send(e_slot, eb.at[me8], eb.at[me8], partner)
    ring_own, ring_other = Ring(comm, ehalf(g), yp, ym), Ring(comm, ehalf(1 - g), yp, ym)
    ring_own.start()
    next(run0)
    comm.recv(e_slot, eb.at[y * 2 + 1 - g], partner)
    ring_other.start()
    ring_own.forward()
    next(run0)
    ring_own.near()
    next(run0)
    ring_other.forward()
    ring_own.far()
    next(run0)
    ring_other.near()
    ring_other.far()
    next(run0)

    def esum(i, carry):
        v = eb[i].astype(F32)
        return carry + jnp.sum(v * v, axis=1, keepdims=True)

    inv_enc = lax.rsqrt(lax.fori_loop(0, 8, esum, jnp.zeros((ROWS, 1), F32)) / FEATURES + EPSILON)

    for h in range(2):

        def norm_enc(i, carry, h=h):
            gain = gb[i, 0, 1:2, h * HALF : (h + 1) * HALF]
            en[i * 2 + h] = (eb[i * 2 + h].astype(F32) * inv_enc * gain).astype(BF)
            return carry

        lax.fori_loop(0, 4, norm_enc, 0)

    for _ in range(3):
        next(run0)
    for rz in range(4):
        st0["wait"](rz)

    acc2[...] = jnp.zeros_like(acc2)

    def project_enc(i, carry):
        acc2[...] += nn(en[i], w0[pl.ds(pl.multiple_of(i * HALF, HALF), HALF), :])
        return carry

    lax.fori_loop(0, 8, project_enc, 0)
    nkv[...] = acc2[...].astype(BF)

    mx_slot = comm.alloc(1)
    rowdot = jnp.zeros((ROWS, 1), F32)
    for i in range(HEADS):
        q, k, v = dq[:, head(i)], nkv[:, head(i)], nkv[:, head(i, True)]
        ct = cot[:, mine_head(i)]
        probs = softmax(nt(q, k), dec_mask)
        rounded = probs.astype(BF)
        mxs[:, head(i)] = nn(rounded, v).astype(BF)
        grad_values = tn(rounded, ct)
        grad_probs = nt(ct, v)
        grad_scores = probs * (grad_probs - jnp.sum(grad_probs * probs, axis=-1, keepdims=True))
        grad_keys = tn(grad_scores.astype(BF), q) * SCALE
        rowdot = rowdot + jnp.sum(
            grad_keys * k.astype(F32) + grad_values * v.astype(F32), axis=1, keepdims=True
        )
        g2[:, head(i)] = grad_keys.astype(BF)
        g2[:, head(i, True)] = grad_values.astype(BF)
    mx_copy = comm.copy(mx_slot, mxs, mxr, partner)

    rd[y] = as_row(rowdot)
    rd_base = comm.alloc(4)
    small_start(rd, rd_base)

    def back_enc(r, h):
        b = mod4(y + r) * 2 + h
        rows = pl.ds(pl.multiple_of(b * HALF, HALF), HALF)
        pb[b] = nt(g2[...], w0[rows, :]).astype(BF)

    def scatter_of(h, j):
        return Scatter(
            comm,
            lambda r: pb.at[mod4(y + r) * 2 + h],
            (rba.at[j, 0], rba.at[j, 1], rbb.at[j, 0], rbb.at[j, 1]),
            yp, ym, ROWS,
        )

    away, home = scatter_of(1 - g, 0), scatter_of(g, 1)
    back_enc(2, 1 - g)
    away.first()
    back_enc(1, 1 - g)
    back_enc(-1, 1 - g)
    away.second()
    back_enc(2, g)
    home.first()
    back_enc(1, g)
    back_enc(-1, g)
    away.third()
    home.second()

    @pl.when(g == 1)
    def _():
        mx_copy.start()

    back_enc(0, 1 - g)
    back_enc(0, g)
    small_wait(rd, rd_base)
    rdp[0] = rd[0] + rd[1] + rd[2] + rd[3]
    comm.send(rd_base + 3, rdp.at[0], rdp.at[1], partner)
    ysum[...] = away.total().astype(BF)
    r3_slot = comm.alloc(1)
    comm.send(r3_slot, ysum, r3, partner)
    home.third()
    grad_in = home.total()
    comm.recv(rd_base + 3, rdp.at[1], partner)
    dot_all = as_col(rdp[0] + rdp[1])
    comm.recv(r3_slot, r3, partner)
    grad_in = grad_in + r3[...].astype(F32)
    grad_enc = (
        inv_enc * gb[y, 0, 1:2, mine] * grad_in
        - eb[me8].astype(F32) * (inv_enc * inv_enc * dot_all / FEATURES)
    ).astype(BF)

    rowdot1 = jnp.zeros((TOK, 1), F32)
    for i in range(HEADS):
        q, k, v = qe[:, head(i)], skv[:, head(i)], skv[:, head(i, True)]
        go = grad_enc[:, head(i)]
        probs = pe[i]
        grad_values = tn(probs.astype(BF), go)
        grad_probs = nt(go, v)
        grad_scores = probs * (grad_probs - jnp.sum(grad_probs * probs, axis=-1, keepdims=True))
        grad_keys = tn(grad_scores.astype(BF), q) * SCALE
        rowdot1 = rowdot1 + jnp.sum(
            grad_keys * k.astype(F32) + grad_values * v.astype(F32), axis=1, keepdims=True
        )
        g1[:, head(i)] = grad_keys.astype(BF)
        g1[:, head(i, True)] = grad_values.astype(BF)

    rd1[y] = as_row(rowdot1)
    rd1_base = comm.alloc(4)
    small_start(rd1, rd1_base)

    def back_state(r, h):
        b = mod4(y + r) * 2 + h
        rows = pl.ds(pl.multiple_of(b * HALF, HALF), HALF)
        pb1[b] = nt(g1[...], w1[rows, :]).astype(BF)

    def scatter_state(h):
        return Scatter(
            comm,
            lambda r: pb1.at[mod4(y + r) * 2 + h],
            (rca.at[h, 0], rca.at[h, 1], rcb.at[h, 0], rcb.at[h, 1]),
            yp, ym, TOK,
        )

    sc = [scatter_state(0), scatter_state(1)]
    for h in range(2):
        back_state(2, h)
        sc[h].first()
        back_state(1, h)
        back_state(-1, h)
        sc[h].second()
    sc[0].third()
    back_state(0, 0)
    back_state(0, 1)
    sc[1].third()
    small_wait(rd1, rd1_base)
    rdp1[0] = rd1[0] + rd1[1] + rd1[2] + rd1[3]
    comm.send(rd1_base + 3, rdp1.at[0], rdp1.at[1], partner)
    t3_slot = comm.alloc(2)
    t3_copies = [comm.copy(t3_slot + h, ysum1.at[h], t3.at[h], partner) for h in range(2)]
    for h in range(2):
        ysum1[h] = sc[h].total().astype(BF)

        @pl.when(g == 0)
        def _(h=h):
            t3_copies[h].start()

    comm.recv(rd1_base + 3, rdp1.at[1], partner)

    @pl.when(g == 0)
    def _():
        mx_copy.wait_recv()
        for h in range(2):
            theirs = mxr if h == 1 else mxs
            cols = slice(h * HALF, (h + 1) * HALF)
            out[:, cols] = states[:, cols].astype(F32) + theirs[...].astype(F32)
        for copy in t3_copies:
            copy.wait_send()

    @pl.when(g == 1)
    def _():
        dot_state = as_col(rdp1[0] + rdp1[1])
        factor = inv_state * inv_state * dot_state / FEATURES
        for h in range(2):
            t3_copies[h].wait_recv()
            cols = slice(h * HALF, (h + 1) * HALF)
            total = ysum1[h].astype(F32) + t3[h].astype(F32)
            out[:, cols] = (
                inv_state * gb[y, 1, 0:1, cols] * total - states[:, cols].astype(F32) * factor
            )
        mx_copy.wait_send()

    comm.drain()
    done1()
    done0()


def per_device(states, neighbours, cotangent, span_of, counts, kv_weight, gains):
    wsrc = kv_weight.reshape(TOK, 2, 2, HALF).transpose(2, 0, 1, 3).reshape(2, TOK, COLS)
    vmem, smem, hbm = (
        pl.BlockSpec(memory_space=m) for m in (pltpu.VMEM, pltpu.SMEM, pl.ANY)
    )

    def bf(*shape):
        return pltpu.VMEM(shape, BF)

    def f32(*shape):
        return pltpu.VMEM(shape, F32)

    scratch = [
        bf(FEATURES, COLS),
        bf(FEATURES, COLS),
        bf(4, TOK, COLS),
        bf(4, TOK, COLS),
        f32(4, 2, 8, COLS),
        f32(4, 8, ROWS),
        bf(8, ROWS, HALF),
        bf(8, ROWS, HALF),
        f32(TOK, COLS),
        bf(TOK, COLS),
        bf(ROWS, HALF),
        f32(HEADS, ROWS, TOK),
        f32(ROWS, COLS),
        bf(ROWS, COLS),
        bf(TOK, HALF),
        bf(ROWS, COLS),
        bf(8, ROWS, HALF),
        bf(2, 2, ROWS // 2, HALF),
        bf(2, 2, ROWS, HALF),
        bf(ROWS, HALF),
        bf(ROWS, HALF),
        bf(TOK, COLS),
        bf(8, TOK, HALF),
        bf(2, 2, TOK // 2, HALF),
        bf(2, 2, TOK, HALF),
        bf(2, TOK, HALF),
        bf(2, TOK, HALF),
        f32(4, 8, ROWS),
        f32(2, 8, ROWS),
        f32(4, 8, TOK),
        f32(2, 8, TOK),
        bf(TOK, HALF),
        bf(TOK, HALF),
        pltpu.SemaphoreType.DMA((SEMS,)),
        pltpu.SemaphoreType.DMA((SEMS,)),
        pltpu.SemaphoreType.DMA((2,)),
    ]
    result = pl.pallas_call(
        kernel,
        out_shape=jax.ShapeDtypeStruct((TOK, COLS), F32),
        in_specs=[hbm, vmem, vmem, vmem, smem, smem, vmem],
        out_specs=vmem,
        scratch_shapes=scratch,
        compiler_params=pltpu.CompilerParams(
            collective_id=0, has_side_effects=True, vmem_limit_bytes=60 * 1024 * 1024
        ),
        name="spanned_attention",
    )(
        wsrc,
        states,
        neighbours.reshape(ROWS, COLS),
        cotangent,
        span_of,
        counts,
        gains.reshape(2, COLS),
    )
    return result[None]


def solution(mesh):
    return jax.shard_map(
        per_device,
        mesh=mesh,
        in_specs=(
            P("dp", "mp"),
            P("dp", None, "mp"),
            P("dp", "mp"),
            P("dp"),
            P("dp"),
            P("group", "dp", None, "mp"),
            P("group", None, "mp"),
        ),
        out_specs=P("group", "dp", "mp"),
        check_vma=False,
    )
```

```python
import functools

import jax
import jax.numpy as jnp
from jax import lax
from jax.experimental import pallas as pl
from jax.experimental.pallas import tpu as pltpu
from jax.sharding import PartitionSpec as P

HD = 128
FEATURES = 4096
CH = 64
EPSILON = 1e-05
NEG_LARGE = -1e30
TOK = 128
ROWS = 256
COLS = 1024
HALF = 512
HEADS = 4
SCALE = HD ** (-0.5)
BF = jnp.bfloat16
F32 = jnp.float32
SEMS = 224


def nt(a, b):
    return lax.dot_general(a, b, (((1,), (1,)), ((), ())), preferred_element_type=F32)


def nn(a, b):
    return lax.dot_general(a, b, (((1,), (0,)), ((), ())), preferred_element_type=F32)


def tn(a, b):
    return lax.dot_general(a, b, (((0,), (0,)), ((), ())), preferred_element_type=F32)


class Comm:
    def __init__(self, ssem, rsem):
        self.ssem, self.rsem = ssem, rsem
        self.used, self.sent = 0, []

    def alloc(self, count):
        base = self.used
        self.used += count
        assert self.used <= SEMS
        return base

    def copy(self, slot, src, dst, dev):
        return pltpu.make_async_remote_copy(
            src_ref=src,
            dst_ref=dst,
            send_sem=self.ssem.at[slot],
            recv_sem=self.rsem.at[slot],
            device_id=dev,
            device_id_type=pl.DeviceIdType.MESH,
        )

    def send(self, slot, src, dst, dev):
        copy = self.copy(slot, src, dst, dev)
        copy.start()
        self.sent.append(copy)

    def recv(self, slot, dst, dev):
        self.copy(slot, dst, dst, dev).wait_recv()

    def drain(self):
        for copy in self.sent:
            copy.wait_send()


class Ring:
    def __init__(self, comm, half, plus, minus):
        self.comm, self.half, self.plus, self.minus = comm, half, plus, minus
        self.base = comm.alloc(6)

    def start(self):
        for slot, k, dev in ((0, 0, self.plus), (2, 1, self.minus), (1, 1, self.plus), (3, 0, self.minus)):
            self.comm.send(self.base + slot, self.half(0, k), self.half(0, k), dev)

    def forward(self):
        self.comm.recv(self.base, self.half(-1, 0), self.minus)
        self.comm.send(self.base + 4, self.half(-1, 0), self.half(-1, 0), self.plus)
        self.comm.recv(self.base + 2, self.half(1, 1), self.plus)
        self.comm.send(self.base + 5, self.half(1, 1), self.half(1, 1), self.minus)

    def near(self):
        self.comm.recv(self.base + 1, self.half(-1, 1), self.minus)
        self.comm.recv(self.base + 3, self.half(1, 0), self.plus)

    def far(self):
        self.comm.recv(self.base + 4, self.half(2, 0), self.minus)
        self.comm.recv(self.base + 5, self.half(2, 1), self.plus)


class Scatter:
    def __init__(self, comm, part, bufs, plus, minus, rows):
        self.comm, self.part, self.plus, self.minus, self.n = comm, part, plus, minus, rows // 2
        self.from_minus, self.from_plus, self.last_minus, self.last_plus = bufs
        self.base = comm.alloc(6)

    def lo(self, ref):
        return ref.at[pl.ds(0, self.n), :]

    def hi(self, ref):
        return ref.at[pl.ds(self.n, self.n), :]

    def first(self):
        self.comm.send(self.base, self.lo(self.part(2)), self.from_minus, self.plus)
        self.comm.send(self.base + 1, self.hi(self.part(2)), self.from_plus, self.minus)

    def second(self):
        self.comm.send(self.base + 2, self.hi(self.part(1)), self.hi(self.last_minus), self.plus)
        self.comm.send(self.base + 3, self.lo(self.part(-1)), self.lo(self.last_plus), self.minus)

    def third(self):
        self.comm.recv(self.base, self.from_minus, self.minus)
        a = self.lo(self.part(1))
        a[...] = (a[...].astype(F32) + self.from_minus[...].astype(F32)).astype(BF)
        self.comm.send(self.base + 4, a, self.lo(self.last_minus), self.plus)
        self.comm.recv(self.base + 1, self.from_plus, self.plus)
        b = self.hi(self.part(-1))
        b[...] = (b[...].astype(F32) + self.from_plus[...].astype(F32)).astype(BF)
        self.comm.send(self.base + 5, b, self.hi(self.last_plus), self.minus)

    def total(self):
        self.comm.recv(self.base + 2, self.hi(self.last_minus), self.minus)
        self.comm.recv(self.base + 3, self.lo(self.last_plus), self.plus)
        self.comm.recv(self.base + 4, self.lo(self.last_minus), self.minus)
        self.comm.recv(self.base + 5, self.hi(self.last_plus), self.plus)
        return (
            self.part(0)[...].astype(F32)
            + self.last_minus[...].astype(F32)
            + self.last_plus[...].astype(F32)
        )


def as_row(col):
    return jnp.transpose(jnp.broadcast_to(col, (col.shape[0], 128)))[0:8, :]


def as_col(row):
    return jnp.transpose(jnp.broadcast_to(row[0:1, :], (128, row.shape[1])))[:, 0:1]


def kernel(
    keys, values, states_in, neigh_in, cot_in, span, counts, gains, out,
    w, theirs, states, neigh, cot, sx, xn, gb, ns, eb, en, acc1, skv, qe, pe, acc2, nkv, dq, g2, pb, rba, rbb, r3, ysum,
    g1, pb1, rca, rcb, t3, ysum1, rd, rdp, rd1, rdp1, mxs, mxr,
    ssem, rsem, lsem,
):
    g = lax.axis_index("group")
    d = lax.axis_index("dp")
    y = lax.axis_index("mp")
    x, zh, c = d // 8, (d // 2) % 4, d % 2
    comm = Comm(ssem, rsem)

    def mod4(v):
        return (v + 4) % 4

    def at_x(r):
        return {"dp": mod4(x + r) * 8 + zh * 2 + c}

    def at_z(r):
        return {"dp": x * 8 + mod4(zh + r) * 2 + c}

    def at_y(r):
        return {"mp": mod4(y + r)}

    partner = {"group": 1 - g}
    sibling = {"dp": d + 1 - 2 * c}
    xp, xm, zp, zm, yp, ym, y2 = at_x(1), at_x(-1), at_z(1), at_z(-1), at_y(1), at_y(-1), at_y(2)

    across = {"group": 1 - g, "dp": x * 8 + mod4(zh + 2 * g - 1) * 2 + c}
    fetch = [
        pltpu.make_async_copy(src, dst, lsem.at[i])
        for i, (src, dst) in enumerate(((states_in, states), (neigh_in, neigh), (cot_in, cot)))
    ]
    own_start = pl.multiple_of(d * TOK, TOK)
    local = []
    for i, (src, grp, dst) in enumerate(
        (src, grp, dst)
        for grp, dst in ((g, w.at[g, pl.ds(own_start, TOK), :]), (1 - g, theirs))
        for src in (keys, values)
    ):
        cols = pl.ds(pl.multiple_of(grp * HALF, HALF), HALF)
        to = dst.at[:, pl.ds((i % 2) * HALF, HALF)]
        local.append(pltpu.make_async_copy(src.at[:, cols], to, lsem.at[3 + i]))
        local[-1].start()
    for copy in fetch:
        copy.start()
    barrier = pltpu.get_barrier_semaphore()
    peers = (partner, sibling, xp, xm, zp, zm, yp, ym, y2, across)
    for dev in peers:
        pl.semaphore_signal(barrier, inc=1, device_id=dev, device_id_type=pl.DeviceIdType.MESH)
    pl.semaphore_wait(barrier, len(peers))

    def wrow(rx, rz, core):
        return pl.multiple_of((mod4(x + rx) * 8 + mod4(zh + rz) * 2 + core) * TOK, TOK)

    own_rows = pl.ds(wrow(0, 0, c), TOK)
    ORDER = {1: (0, -1, 1, 2), 0: (0, 1, -1, 2)}
    PLAN = {
        1: [(1, 0), (1, 1), (1, 2), (1, 3), (0, 0), (0, 1), (0, 2), (0, 3)],
        0: [(0, 0), (1, 0), (1, 1), (1, 2), (1, 3), (0, 1), (0, 2), (0, 3)],
    }
    zbase = {m: comm.alloc(10) for m in (0, 1)}
    zsent = {0: [], 1: []}

    def either(fn):
        for grp in (0, 1):
            pl.when(g == grp)(functools.partial(fn, grp))

    def zblock(m, rz):
        return w.at[m, pl.ds(wrow(0, rz, c), TOK), :]

    def zhalf(m, rz, k):
        return w.at[m, pl.ds(pl.multiple_of(wrow(0, rz, c) + k * 64, 64), 64), :]

    def zsend(grp, slot, ref, dev, src=None):
        def make():
            dst = ref()
            return comm.copy(slot, dst if src is None else src(), dst, dev)

        make().start()
        zsent[grp].append(make)

    def zout(grp):
        m, base = grp, zbase[grp]
        for slot, dev in ((6, partner), (7, across)):
            zsend(grp, base + slot, lambda: zblock(m, 0), dev, lambda: theirs)
        for slot, k, dev in ((0, 0, zp), (2, 1, zm), (1, 1, zp), (3, 0, zm)):
            zsend(grp, base + slot, lambda k=k: zhalf(m, 0, k), dev)

    def zarrive(grp, m, i):
        base, rz = zbase[m], ORDER[m][i]
        if grp == m:
            if i == 0:
                return
            if i == 1:
                comm.recv(base, zhalf(m, -1, 0), zm)
                zsend(grp, base + 4, lambda: zhalf(m, -1, 0), zp)
                comm.recv(base + 2, zhalf(m, 1, 1), zp)
                zsend(grp, base + 5, lambda: zhalf(m, 1, 1), zm)
            if rz == -1:
                comm.recv(base + 1, zhalf(m, -1, 1), zm)
            elif rz == 1:
                comm.recv(base + 3, zhalf(m, 1, 0), zp)
            else:
                comm.recv(base + 4, zhalf(m, 2, 0), zm)
                comm.recv(base + 5, zhalf(m, 2, 1), zp)
            return
        if i == 0:
            comm.recv(base + 6, zblock(m, 0), partner)
            zsend(grp, base + 8, lambda: zblock(m, 0), zm if m == 1 else zp)
        elif i == 1:
            comm.recv(base + 7, zblock(m, rz), across)
            zsend(grp, base + 9, lambda: zblock(m, rz), zp if m == 1 else zm)
        else:
            comm.recv(base + 6 + i, zblock(m, rz), zp)

    def plan(grp, s):
        m, i = PLAN[grp][s]
        return m, ORDER[m][i]

    class Slot:
        def __init__(self, s):
            (m0, r0), (m1, r1) = plan(0, s), plan(1, s)
            self.s, self.m, self.rz = s, m0 + (m1 - m0) * g, r0 + (r1 - r0) * g
            self.ring = Ring(comm, self.half, xp, xm)
            self.sib = comm.alloc(4)

        def half(self, r, k):
            return w.at[self.m, pl.ds(pl.multiple_of(wrow(r, self.rz, c) + k * 64, 64), 64), :]

        def share(self, *rels):
            for rx in rels:
                block = w.at[self.m, pl.ds(wrow(rx, self.rz, c), TOK), :]
                comm.send(self.sib + rx % 4, block, block, sibling)

        def start(self):
            either(lambda grp: zarrive(grp, *PLAN[grp][self.s]))
            self.ring.start()
            self.share(0)

        def forward(self):
            self.ring.forward()

        def rest(self):
            self.ring.near()
            self.share(-1, 1)
            self.ring.far()
            self.share(2)

    slots = [Slot(s) for s in range(8)]
    sib_first = slots[0].sib
    sib_step = slots[1].sib - slots[0].sib

    def shared(m, i):
        s0, s1 = (PLAN[grp].index((m, i)) for grp in (0, 1))
        rz = ORDER[m][i]
        for rx in range(4):
            comm.recv(
                sib_first + (s0 + (s1 - s0) * g) * sib_step + rx,
                w.at[m, pl.ds(wrow(rx, rz, 1 - c), TOK), :],
                sibling,
            )

    for copy in local:
        copy.wait()
    pl.when(g == 1)(lambda: zout(1))
    slots[0].start()

    def shalf(r, k):
        return sx.at[mod4(y + r), pl.ds(k * 64, 64), :]

    for copy in fetch:
        copy.wait()
    sx[y] = states[...]
    even = lax.broadcasted_iota(jnp.int32, (8, COLS), 0) % 2 == 0
    gb[y, g] = jnp.where(even, gains[0:1, :], gains[1:2, :])
    sring = Ring(comm, shalf, yp, ym)
    sring.start()
    gain_slot = comm.alloc(4)
    comm.send(gain_slot, gb.at[y, g], gb.at[y, g], partner)

    def small_start(buf, base):
        for i, (r, dev) in enumerate(((1, yp), (-1, ym), (2, y2))):
            comm.send(base + i, buf.at[y], buf.at[y], dev)

    def small_wait(buf, base):
        for i, (r, dev) in enumerate(((-1, ym), (1, yp), (2, y2))):
            comm.recv(base + i, buf.at[mod4(y + r)], dev)

    nf = neigh[...].astype(F32)
    ns[y] = as_row(jnp.sum(nf * nf, axis=1, keepdims=True))
    ns_base = comm.alloc(3)
    small_start(ns, ns_base)
    comm.recv(gain_slot, gb.at[y, 1 - g], partner)
    small_start(gb, gain_slot + 1)
    slots[0].forward()
    sring.forward()
    slots[1].start()
    slots[0].rest()
    sring.near()
    sring.far()
    small_wait(ns, ns_base)
    small_wait(gb, gain_slot + 1)

    mine = pl.ds(pl.multiple_of(g * HALF, HALF), HALF)
    sums = jnp.zeros((TOK, 1), F32)
    for i in range(4):
        v = sx[i].astype(F32)
        sums = sums + jnp.sum(v * v, axis=1, keepdims=True)
    inv_state = lax.rsqrt(sums / FEATURES + EPSILON)

    def norm_states(i, carry):
        xn[i] = (sx[i].astype(F32) * inv_state * gb[i, 1, 0:1, :]).astype(BF)
        return carry

    lax.fori_loop(0, 4, norm_states, 0)
    dq[...] = (states[:, mine].astype(F32) * inv_state * gb[y, 0, 0:1, mine]).astype(BF)
    inv_neigh = as_col(lax.rsqrt((ns[0] + ns[1] + ns[2] + ns[3]) / FEATURES + EPSILON))
    qe[...] = (neigh[:, mine].astype(F32) * inv_neigh * gb[y, 1, 1:2, mine]).astype(BF)

    def chunk_rows(i, z):
        return pl.ds(pl.multiple_of((i * 4 + z) * 256, 256), 256)

    def project_states(i):
        shared(1, i)
        z = mod4(zh + ORDER[1][i])

        def step(k, carry):
            part = nn(xn[k, :, pl.ds(pl.multiple_of(z * 256, 256), 256)], w[1, chunk_rows(k, z), :])
            acc1[...] += part
            return carry

        lax.fori_loop(0, 4, step, 0)

    acc1[...] = jnp.zeros_like(acc1)
    slots[1].forward()
    slots[2].start()
    slots[1].rest()
    pl.when(g == 0)(lambda: zout(0))
    project_states(0)
    slots[2].forward()
    slots[3].start()
    slots[2].rest()
    project_states(1)
    slots[3].forward()
    slots[4].start()
    slots[3].rest()
    project_states(2)
    slots[4].forward()
    slots[5].start()
    slots[4].rest()
    project_states(3)
    skv[...] = acc1[...].astype(BF)

    base_span = d * 2

    def spans_of(slot):
        spans = [span[i] - base_span for i in range(4)]
        return jnp.where(
            slot == 0, spans[0], jnp.where(slot == 1, spans[1], jnp.where(slot == 2, spans[2], spans[3]))
        )

    def iota(shape, axis):
        return lax.broadcasted_iota(jnp.int32, shape, axis)

    enc_mask = spans_of(iota((ROWS, TOK), 0) >> 6) == (iota((ROWS, TOK), 1) >> 6)
    slots_t = iota((TOK, ROWS), 1) >> 6
    dec_mask = (spans_of(slots_t) == (iota((TOK, ROWS), 0) >> 6)) & (slots_t < counts[0])

    def softmax(scores, mask):
        scores = jnp.where(mask, scores * SCALE, NEG_LARGE)
        top = jnp.max(scores, axis=-1, keepdims=True)
        raised = jnp.where(mask, jnp.exp(scores - top), 0.0)
        return raised / jnp.sum(raised, axis=-1, keepdims=True)

    def head(i, second=False):
        start = i * HD + (HALF if second else 0)
        return slice(start, start + HD)

    def mine_head(i):
        return pl.ds(pl.multiple_of(g * HALF + i * HD, HD), HD)

    me8 = y * 2 + g
    for i in range(HEADS):
        probs = softmax(nt(qe[:, head(i)], skv[:, head(i)]), enc_mask)
        pe[i] = probs
        o = nn(probs.astype(BF), skv[:, head(i, True)])
        eb[me8, :, head(i)] = (neigh[:, mine_head(i)].astype(F32) + o).astype(BF)

    def ehalf(grp):
        return lambda r, k: eb.at[mod4(y + r) * 2 + grp, pl.ds(k * 128, 128), :]

    e_slot = comm.alloc(1)
    comm.send(e_slot, eb.at[me8], eb.at[me8], partner)
    ring_own, ring_other = Ring(comm, ehalf(g), yp, ym), Ring(comm, ehalf(1 - g), yp, ym)
    ring_own.start()
    slots[5].forward()
    slots[6].start()
    comm.recv(e_slot, eb.at[y * 2 + 1 - g], partner)
    ring_other.start()
    ring_own.forward()
    slots[5].rest()
    ring_own.near()
    slots[6].forward()
    slots[7].start()
    ring_other.forward()
    ring_own.far()
    slots[6].rest()
    ring_other.near()
    ring_other.far()
    slots[7].forward()

    def esum(i, carry):
        v = eb[i].astype(F32)
        return carry + jnp.sum(v * v, axis=1, keepdims=True)

    inv_enc = lax.rsqrt(lax.fori_loop(0, 8, esum, jnp.zeros((ROWS, 1), F32)) / FEATURES + EPSILON)

    for h in range(2):

        def norm_enc(i, carry, h=h):
            gain = gb[i, 0, 1:2, h * HALF : (h + 1) * HALF]
            en[i * 2 + h] = (eb[i * 2 + h].astype(F32) * inv_enc * gain).astype(BF)
            return carry

        lax.fori_loop(0, 4, norm_enc, 0)

    acc2[...] = jnp.zeros_like(acc2)

    def project_enc(i):
        shared(0, i)
        z = mod4(zh + ORDER[0][i])

        def step(k, carry):
            cols = pl.ds(pl.multiple_of((z % 2) * 256, 256), 256)
            acc2[...] += nn(en[k * 2 + z // 2, :, cols], w[0, chunk_rows(k, z), :])
            return carry

        lax.fori_loop(0, 4, step, 0)

    for i in range(3):
        project_enc(i)
    slots[7].rest()
    project_enc(3)
    nkv[...] = acc2[...].astype(BF)

    mx_slot = comm.alloc(1)
    rowdot = jnp.zeros((ROWS, 1), F32)
    for i in range(HEADS):
        q, k, v = dq[:, head(i)], nkv[:, head(i)], nkv[:, head(i, True)]
        ct = cot[:, mine_head(i)]
        probs = softmax(nt(q, k), dec_mask)
        rounded = probs.astype(BF)
        mxs[:, head(i)] = nn(rounded, v).astype(BF)
        grad_values = tn(rounded, ct)
        grad_probs = nt(ct, v)
        grad_scores = probs * (grad_probs - jnp.sum(grad_probs * probs, axis=-1, keepdims=True))
        grad_keys = tn(grad_scores.astype(BF), q) * SCALE
        rowdot = rowdot + jnp.sum(
            grad_keys * k.astype(F32) + grad_values * v.astype(F32), axis=1, keepdims=True
        )
        g2[:, head(i)] = grad_keys.astype(BF)
        g2[:, head(i, True)] = grad_values.astype(BF)
    mx_copy = comm.copy(mx_slot, mxs, mxr, partner)

    rd[y] = as_row(rowdot)
    rd_base = comm.alloc(4)
    small_start(rd, rd_base)

    def back_enc(r, h):
        b = mod4(y + r) * 2 + h
        rows = pl.ds(pl.multiple_of(b * HALF, HALF), HALF)
        pb[b] = nt(g2[...], w[0, rows, :]).astype(BF)

    def scatter_of(h, j):
        return Scatter(
            comm,
            lambda r: pb.at[mod4(y + r) * 2 + h],
            (rba.at[j, 0], rba.at[j, 1], rbb.at[j, 0], rbb.at[j, 1]),
            yp, ym, ROWS,
        )

    away, home = scatter_of(1 - g, 0), scatter_of(g, 1)
    back_enc(2, 1 - g)
    away.first()
    back_enc(1, 1 - g)
    back_enc(-1, 1 - g)
    away.second()
    back_enc(2, g)
    home.first()
    back_enc(1, g)
    back_enc(-1, g)
    away.third()
    home.second()

    @pl.when(g == 1)
    def _():
        mx_copy.start()

    back_enc(0, 1 - g)
    back_enc(0, g)
    small_wait(rd, rd_base)
    rdp[0] = rd[0] + rd[1] + rd[2] + rd[3]
    comm.send(rd_base + 3, rdp.at[0], rdp.at[1], partner)
    ysum[...] = away.total().astype(BF)
    r3_slot = comm.alloc(1)
    comm.send(r3_slot, ysum, r3, partner)
    home.third()
    grad_in = home.total()
    comm.recv(rd_base + 3, rdp.at[1], partner)
    dot_all = as_col(rdp[0] + rdp[1])
    comm.recv(r3_slot, r3, partner)
    grad_in = grad_in + r3[...].astype(F32)
    grad_enc = (
        inv_enc * gb[y, 0, 1:2, mine] * grad_in
        - eb[me8].astype(F32) * (inv_enc * inv_enc * dot_all / FEATURES)
    ).astype(BF)

    rowdot1 = jnp.zeros((TOK, 1), F32)
    for i in range(HEADS):
        q, k, v = qe[:, head(i)], skv[:, head(i)], skv[:, head(i, True)]
        go = grad_enc[:, head(i)]
        probs = pe[i]
        grad_values = tn(probs.astype(BF), go)
        grad_probs = nt(go, v)
        grad_scores = probs * (grad_probs - jnp.sum(grad_probs * probs, axis=-1, keepdims=True))
        grad_keys = tn(grad_scores.astype(BF), q) * SCALE
        rowdot1 = rowdot1 + jnp.sum(
            grad_keys * k.astype(F32) + grad_values * v.astype(F32), axis=1, keepdims=True
        )
        g1[:, head(i)] = grad_keys.astype(BF)
        g1[:, head(i, True)] = grad_values.astype(BF)

    rd1[y] = as_row(rowdot1)
    rd1_base = comm.alloc(4)
    small_start(rd1, rd1_base)

    def back_state(r, h):
        b = mod4(y + r) * 2 + h
        rows = pl.ds(pl.multiple_of(b * HALF, HALF), HALF)
        pb1[b] = nt(g1[...], w[1, rows, :]).astype(BF)

    def scatter_state(h):
        return Scatter(
            comm,
            lambda r: pb1.at[mod4(y + r) * 2 + h],
            (rca.at[h, 0], rca.at[h, 1], rcb.at[h, 0], rcb.at[h, 1]),
            yp, ym, TOK,
        )

    sc = [scatter_state(0), scatter_state(1)]
    for h in range(2):
        back_state(2, h)
        sc[h].first()
        back_state(1, h)
        back_state(-1, h)
        sc[h].second()
    sc[0].third()
    back_state(0, 0)
    back_state(0, 1)
    sc[1].third()
    small_wait(rd1, rd1_base)
    rdp1[0] = rd1[0] + rd1[1] + rd1[2] + rd1[3]
    comm.send(rd1_base + 3, rdp1.at[0], rdp1.at[1], partner)
    t3_slot = comm.alloc(2)
    t3_copies = [comm.copy(t3_slot + h, ysum1.at[h], t3.at[h], partner) for h in range(2)]
    for h in range(2):
        ysum1[h] = sc[h].total().astype(BF)

        @pl.when(g == 0)
        def _(h=h):
            t3_copies[h].start()

    comm.recv(rd1_base + 3, rdp1.at[1], partner)

    @pl.when(g == 0)
    def _():
        mx_copy.wait_recv()
        for h in range(2):
            heads_out = mxr if h == 1 else mxs
            cols = slice(h * HALF, (h + 1) * HALF)
            out[:, cols] = states[:, cols].astype(F32) + heads_out[...].astype(F32)
        for copy in t3_copies:
            copy.wait_send()

    @pl.when(g == 1)
    def _():
        dot_state = as_col(rdp1[0] + rdp1[1])
        factor = inv_state * inv_state * dot_state / FEATURES
        for h in range(2):
            t3_copies[h].wait_recv()
            cols = slice(h * HALF, (h + 1) * HALF)
            total = ysum1[h].astype(F32) + t3[h].astype(F32)
            out[:, cols] = (
                inv_state * gb[y, 1, 0:1, cols] * total - states[:, cols].astype(F32) * factor
            )
        mx_copy.wait_send()

    comm.drain()
    either(lambda grp: [make().wait_send() for make in zsent[grp]] and None)


def per_device(states, neighbours, cotangent, span_of, counts, kv_weight, gains):
    keys, values = kv_weight[0, :, 0, :], kv_weight[0, :, 1, :]
    vmem, smem, hbm = (
        pl.BlockSpec(memory_space=m) for m in (pltpu.VMEM, pltpu.SMEM, pl.ANY)
    )

    def bf(*shape):
        return pltpu.VMEM(shape, BF)

    def f32(*shape):
        return pltpu.VMEM(shape, F32)

    scratch = [
        bf(2, FEATURES, COLS),
        bf(TOK, COLS),
        bf(TOK, COLS),
        bf(ROWS, COLS),
        bf(TOK, COLS),
        bf(4, TOK, COLS),
        bf(4, TOK, COLS),
        f32(4, 2, 8, COLS),
        f32(4, 8, ROWS),
        bf(8, ROWS, HALF),
        bf(8, ROWS, HALF),
        f32(TOK, COLS),
        bf(TOK, COLS),
        bf(ROWS, HALF),
        f32(HEADS, ROWS, TOK),
        f32(ROWS, COLS),
        bf(ROWS, COLS),
        bf(TOK, HALF),
        bf(ROWS, COLS),
        bf(8, ROWS, HALF),
        bf(2, 2, ROWS // 2, HALF),
        bf(2, 2, ROWS, HALF),
        bf(ROWS, HALF),
        bf(ROWS, HALF),
        bf(TOK, COLS),
        bf(8, TOK, HALF),
        bf(2, 2, TOK // 2, HALF),
        bf(2, 2, TOK, HALF),
        bf(2, TOK, HALF),
        bf(2, TOK, HALF),
        f32(4, 8, ROWS),
        f32(2, 8, ROWS),
        f32(4, 8, TOK),
        f32(2, 8, TOK),
        bf(TOK, HALF),
        bf(TOK, HALF),
        pltpu.SemaphoreType.DMA((SEMS,)),
        pltpu.SemaphoreType.DMA((SEMS,)),
        pltpu.SemaphoreType.DMA((7,)),
    ]
    result = pl.pallas_call(
        kernel,
        out_shape=jax.ShapeDtypeStruct((TOK, COLS), F32),
        in_specs=[hbm, hbm, hbm, hbm, hbm, smem, smem, vmem],
        out_specs=vmem,
        scratch_shapes=scratch,
        compiler_params=pltpu.CompilerParams(
            collective_id=0, has_side_effects=True, vmem_limit_bytes=60 * 1024 * 1024
        ),
        name="spanned_attention",
    )(
        keys,
        values,
        states,
        neighbours.reshape(ROWS, COLS),
        cotangent,
        span_of,
        counts,
        gains.reshape(2, COLS),
    )
    return result[None]


def solution(mesh):
    return jax.shard_map(
        per_device,
        mesh=mesh,
        in_specs=(
            P("dp", "mp"),
            P("dp", None, "mp"),
            P("dp", "mp"),
            P("dp"),
            P("dp"),
            P("group", "dp", None, "mp"),
            P("group", None, "mp"),
        ),
        out_specs=P("group", "dp", "mp"),
        check_vma=False,
    )
```

```python
import functools

import jax
import jax.numpy as jnp
from jax import lax
from jax.experimental import pallas as pl
from jax.experimental.pallas import tpu as pltpu
from jax.sharding import PartitionSpec as P

HD = 128
FEATURES = 4096
CH = 64
EPSILON = 1e-05
NEG_LARGE = -1e30
TOK = 128
ROWS = 256
COLS = 1024
HALF = 512
HEADS = 4
SCALE = HD ** (-0.5)
BF = jnp.bfloat16
F32 = jnp.float32
SEMS = 320
AROWS = TOK
SPLIT = 64


def nt(a, b):
    return lax.dot_general(a, b, (((1,), (1,)), ((), ())), preferred_element_type=F32)


def nn(a, b):
    return lax.dot_general(a, b, (((1,), (0,)), ((), ())), preferred_element_type=F32)


def tn(a, b):
    return lax.dot_general(a, b, (((0,), (0,)), ((), ())), preferred_element_type=F32)


class Comm:
    def __init__(self, ssem, rsem):
        self.ssem, self.rsem = ssem, rsem
        self.used, self.sent = 0, []

    def alloc(self, count):
        base = self.used
        self.used += count
        assert self.used <= SEMS
        return base

    def copy(self, slot, src, dst, dev):
        return pltpu.make_async_remote_copy(
            src_ref=src,
            dst_ref=dst,
            send_sem=self.ssem.at[slot],
            recv_sem=self.rsem.at[slot],
            device_id=dev,
            device_id_type=pl.DeviceIdType.MESH,
        )

    def send(self, slot, src, dst, dev):
        copy = self.copy(slot, src, dst, dev)
        copy.start()
        self.sent.append(copy)

    def recv(self, slot, dst, dev):
        self.copy(slot, dst, dst, dev).wait_recv()

    def drain(self):
        for copy in self.sent:
            copy.wait_send()


class Ring:
    def __init__(self, comm, half, plus, minus):
        self.comm, self.half, self.plus, self.minus = comm, half, plus, minus
        self.base = comm.alloc(6)

    def start(self):
        for slot, k, dev in ((0, 0, self.plus), (2, 1, self.minus), (1, 1, self.plus), (3, 0, self.minus)):
            self.comm.send(self.base + slot, self.half(0, k), self.half(0, k), dev)

    def forward(self):
        self.comm.recv(self.base, self.half(-1, 0), self.minus)
        self.comm.send(self.base + 4, self.half(-1, 0), self.half(-1, 0), self.plus)
        self.comm.recv(self.base + 2, self.half(1, 1), self.plus)
        self.comm.send(self.base + 5, self.half(1, 1), self.half(1, 1), self.minus)

    def near(self):
        self.comm.recv(self.base + 1, self.half(-1, 1), self.minus)
        self.comm.recv(self.base + 3, self.half(1, 0), self.plus)

    def far(self):
        self.comm.recv(self.base + 4, self.half(2, 0), self.minus)
        self.comm.recv(self.base + 5, self.half(2, 1), self.plus)


class Scatter:
    def __init__(self, comm, part, bufs, plus, minus, rows):
        self.comm, self.part, self.plus, self.minus, self.n = comm, part, plus, minus, rows // 2
        self.from_minus, self.from_plus, self.last_minus, self.last_plus = bufs
        self.base = comm.alloc(6)

    def lo(self, ref):
        return ref.at[pl.ds(0, self.n), :]

    def hi(self, ref):
        return ref.at[pl.ds(self.n, self.n), :]

    def first(self):
        self.comm.send(self.base, self.lo(self.part(2)), self.from_minus, self.plus)
        self.comm.send(self.base + 1, self.hi(self.part(2)), self.from_plus, self.minus)

    def second(self):
        self.comm.send(self.base + 2, self.hi(self.part(1)), self.hi(self.last_minus), self.plus)
        self.comm.send(self.base + 3, self.lo(self.part(-1)), self.lo(self.last_plus), self.minus)

    def third(self):
        self.comm.recv(self.base, self.from_minus, self.minus)
        a = self.lo(self.part(1))
        a[...] = (a[...].astype(F32) + self.from_minus[...].astype(F32)).astype(BF)
        self.comm.send(self.base + 4, a, self.lo(self.last_minus), self.plus)
        self.comm.recv(self.base + 1, self.from_plus, self.plus)
        b = self.hi(self.part(-1))
        b[...] = (b[...].astype(F32) + self.from_plus[...].astype(F32)).astype(BF)
        self.comm.send(self.base + 5, b, self.hi(self.last_plus), self.minus)

    def total(self):
        self.comm.recv(self.base + 2, self.hi(self.last_minus), self.minus)
        self.comm.recv(self.base + 3, self.lo(self.last_plus), self.plus)
        self.comm.recv(self.base + 4, self.lo(self.last_minus), self.minus)
        self.comm.recv(self.base + 5, self.hi(self.last_plus), self.plus)
        return (
            self.part(0)[...].astype(F32)
            + self.last_minus[...].astype(F32)
            + self.last_plus[...].astype(F32)
        )


def as_row(col):
    return jnp.transpose(jnp.broadcast_to(col, (col.shape[0], 128)))[0:8, :]


def as_col(row):
    return jnp.transpose(jnp.broadcast_to(row[0:1, :], (128, row.shape[1])))[:, 0:1]


def kernel(
    wide, states_in, neigh_in, cot_in, span, counts, gains, out,
    w, theirs, states, neigh, cot, sx, xn, gb, ns, eb, en, acc1, skv, qe, pe, acc2, nkv, dq, g2, pb, lz, rba, rbb, r3, ysum,
    g1, pb1, rca, rcb, t3, ysum1, rd, rdp, rd1, rdp1, mxs, mxr,
    ssem, rsem, lsem,
):
    g = lax.axis_index("group")
    d = lax.axis_index("dp")
    y = lax.axis_index("mp")
    x, zh, c = d // 8, (d // 2) % 4, d % 2
    comm = Comm(ssem, rsem)

    def mod4(v):
        return (v + 4) % 4

    def at_x(r):
        return {"dp": mod4(x + r) * 8 + zh * 2 + c}

    def at_z(r):
        return {"dp": x * 8 + mod4(zh + r) * 2 + c}

    def at_y(r):
        return {"mp": mod4(y + r)}

    partner = {"group": 1 - g}
    sibling = {"dp": d + 1 - 2 * c}
    xp, xm, zp, zm, yp, ym, y2 = at_x(1), at_x(-1), at_z(1), at_z(-1), at_y(1), at_y(-1), at_y(2)

    across = {"group": 1 - g, "dp": x * 8 + mod4(zh + 2 * g - 1) * 2 + c}
    fetch = [
        pltpu.make_async_copy(src, dst, lsem.at[i])
        for i, (src, dst) in enumerate(((states_in, states), (neigh_in, neigh), (cot_in, cot)))
    ]
    local = []
    for i, (grp, dst) in enumerate(((g, w.at[g, x, zh, c]), (1 - g, theirs))):
        for pair in range(2):
            cols = pl.ds(pl.multiple_of(pair * COLS + grp * HALF, HALF), HALF)
            to = dst.at[:, pl.ds(pair * HALF, HALF)]
            local.append(pltpu.make_async_copy(wide.at[:, cols], to, lsem.at[3 + 2 * i + pair]))
            local[-1].start()
    for copy in fetch:
        copy.start()
    barrier = pltpu.get_barrier_semaphore()
    peers = (partner, sibling, xp, xm, zp, zm, yp, ym, y2, across)
    for dev in peers:
        pl.semaphore_signal(barrier, inc=1, device_id=dev, device_id_type=pl.DeviceIdType.MESH)
    for copy in fetch:
        copy.wait()
    nf = neigh[...].astype(F32)
    sq_rows = as_row(jnp.sum(nf * nf, axis=1, keepdims=True))
    sx[y] = states[...]
    even = lax.broadcasted_iota(jnp.int32, (8, COLS), 0) % 2 == 0
    gb[y, g] = jnp.where(even, gains[0:1, :], gains[1:2, :])
    for copy in local:
        copy.wait()
    pl.semaphore_wait(barrier, len(peers))

    ORDER = {1: (0, -1, 1, 2), 0: (0, 1, -1, 2)}
    PLAN = {
        1: [(1, 0), (0, 0), (1, 1), (1, 2), (1, 3), (0, 1), (0, 2), (0, 3)],
        0: [(0, 0), (1, 0), (1, 1), (1, 2), (1, 3), (0, 1), (0, 2), (0, 3)],
    }
    zbase = {m: comm.alloc(10) for m in (0, 1)}
    zsent = {0: [], 1: []}

    def whole(m, rx, rz, core):
        return w.at[m, mod4(x + rx), mod4(zh + rz), core]

    def main(m, rx, rz, core):
        return whole(m, rx, rz, core).at[pl.ds(0, AROWS), :]

    def main_half(m, rx, rz, k):
        rows = pl.ds(0, SPLIT) if k == 0 else pl.ds(SPLIT, AROWS - SPLIT)
        return whole(m, rx, rz, c).at[rows, :]

    def either(fn):
        for grp in (0, 1):
            pl.when(g == grp)(functools.partial(fn, grp))

    def zhalf(m, rz, k):
        return main_half(m, 0, rz, k)

    def zsend(grp, slot, ref, dev, src=None):
        def make():
            dst = ref()
            return comm.copy(slot, dst if src is None else src(), dst, dev)

        make().start()
        zsent[grp].append(make)

    def zpartner(grp):
        zsend(grp, zbase[grp] + 6, lambda: whole(grp, 0, 0, c), partner, lambda: theirs)

    def zout(grp):
        m, base = grp, zbase[grp]
        zsend(
            grp, base + 7, lambda: main(m, 0, 0, c), across, lambda: theirs.at[pl.ds(0, AROWS), :]
        )
        for slot, k, dev in ((0, 0, zp), (2, 1, zm), (1, 1, zp), (3, 0, zm)):
            zsend(grp, base + slot, lambda k=k: zhalf(m, 0, k), dev)

    def zarrive(grp, m, i):
        base, rz = zbase[m], ORDER[m][i]
        if grp == m:
            if i == 0:
                return
            if i == 1:
                comm.recv(base, zhalf(m, -1, 0), zm)
                zsend(grp, base + 4, lambda: zhalf(m, -1, 0), zp)
                comm.recv(base + 2, zhalf(m, 1, 1), zp)
                zsend(grp, base + 5, lambda: zhalf(m, 1, 1), zm)
            if rz == -1:
                comm.recv(base + 1, zhalf(m, -1, 1), zm)
            elif rz == 1:
                comm.recv(base + 3, zhalf(m, 1, 0), zp)
            else:
                comm.recv(base + 4, zhalf(m, 2, 0), zm)
                comm.recv(base + 5, zhalf(m, 2, 1), zp)
            return
        if i == 0:
            comm.recv(base + 6, whole(m, 0, 0, c), partner)
            if m == 1:
                zsend(grp, base + 8, lambda: main(m, 0, 0, c), zm)
        elif i == 1:
            if m == 0:
                zsend(grp, base + 8, lambda: main(m, 0, 0, c), zp)
            comm.recv(base + 7, main(m, 0, rz, c), across)
            zsend(grp, base + 9, lambda: main(m, 0, rz, c), zp if m == 1 else zm)
        else:
            comm.recv(base + 6 + i, main(m, 0, rz, c), zp)

    def plan(grp, s):
        m, i = PLAN[grp][s]
        return m, ORDER[m][i]

    class Slot:
        def __init__(self, s):
            (m0, r0), (m1, r1) = plan(0, s), plan(1, s)
            self.s, self.m, self.rz = s, m0 + (m1 - m0) * g, r0 + (r1 - r0) * g
            self.ring = Ring(comm, self.half, xp, xm)
            self.sib = comm.alloc(4)

        def half(self, r, k):
            return main_half(self.m, r, self.rz, k)

        def share(self, *rels):
            for rx in rels:
                block = main(self.m, rx, self.rz, c)
                comm.send(self.sib + rx % 4, block, block, sibling)

        def start(self):
            either(lambda grp: zarrive(grp, *PLAN[grp][self.s]))
            self.ring.start()
            self.share(0)

        def forward(self):
            self.ring.forward()

        def rest(self):
            self.ring.near()
            self.share(-1, 1)
            self.ring.far()
            self.share(2)

    slots = [Slot(s) for s in range(8)]
    sib_first = slots[0].sib
    sib_step = slots[1].sib - slots[0].sib

    def shared(m, i):
        s0, s1 = (PLAN[grp].index((m, i)) for grp in (0, 1))
        for rx in range(4):
            comm.recv(
                sib_first + (s0 + (s1 - s0) * g) * sib_step + rx,
                main(m, rx, ORDER[m][i], 1 - c),
                sibling,
            )

    either(zpartner)
    slots[0].start()

    def shalf(r, k):
        return sx.at[mod4(y + r), pl.ds(k * 64, 64), :]

    sring = Ring(comm, shalf, yp, ym)
    sring.start()
    gain_slot = comm.alloc(4)
    comm.send(gain_slot, gb.at[y, g], gb.at[y, g], partner)

    def small_start(buf, base):
        for i, (r, dev) in enumerate(((1, yp), (-1, ym), (2, y2))):
            comm.send(base + i, buf.at[y], buf.at[y], dev)

    def small_wait(buf, base):
        for i, (r, dev) in enumerate(((-1, ym), (1, yp), (2, y2))):
            comm.recv(base + i, buf.at[mod4(y + r)], dev)

    slots[0].forward()
    pl.when(g == 1)(lambda: zout(1))
    sring.forward()
    ns[y] = sq_rows
    ns_base = comm.alloc(3)
    small_start(ns, ns_base)
    comm.recv(gain_slot, gb.at[y, 1 - g], partner)
    small_start(gb, gain_slot + 1)
    slots[1].start()
    slots[0].rest()
    sring.near()
    sring.far()
    small_wait(ns, ns_base)
    small_wait(gb, gain_slot + 1)
    slots[1].forward()
    slots[2].start()

    mine = pl.ds(pl.multiple_of(g * HALF, HALF), HALF)
    sums = jnp.zeros((TOK, 1), F32)
    for i in range(4):
        v = sx[i].astype(F32)
        sums = sums + jnp.sum(v * v, axis=1, keepdims=True)
    inv_state = lax.rsqrt(sums / FEATURES + EPSILON)

    def norm_states(i, carry):
        xn[i] = (sx[i].astype(F32) * inv_state * gb[i, 1, 0:1, :]).astype(BF)
        return carry

    lax.fori_loop(0, 4, norm_states, 0)
    dq[...] = (states[:, mine].astype(F32) * inv_state * gb[y, 0, 0:1, mine]).astype(BF)
    inv_neigh = as_col(lax.rsqrt((ns[0] + ns[1] + ns[2] + ns[3]) / FEATURES + EPSILON))
    qe[...] = (neigh[:, mine].astype(F32) * inv_neigh * gb[y, 1, 1:2, mine]).astype(BF)

    def project_states(i):
        shared(1, i)
        z = mod4(zh + ORDER[1][i])

        def step(k, carry):
            part = nn(xn[k, :, pl.ds(pl.multiple_of(z * 256, 256), 256)], w[1, k, z].reshape(256, COLS))
            acc1[...] += part
            return carry

        lax.fori_loop(0, 4, step, 0)

    acc1[...] = jnp.zeros_like(acc1)
    slots[1].rest()
    slots[2].forward()
    slots[3].start()
    pl.when(g == 0)(lambda: zout(0))
    slots[2].rest()
    slots[3].forward()
    slots[4].start()
    slots[3].rest()
    slots[4].forward()
    slots[5].start()
    project_states(0)
    project_states(1)
    project_states(2)
    slots[4].rest()
    project_states(3)
    skv[...] = acc1[...].astype(BF)

    base_span = d * 2

    def spans_of(slot):
        spans = [span[i] - base_span for i in range(4)]
        return jnp.where(
            slot == 0, spans[0], jnp.where(slot == 1, spans[1], jnp.where(slot == 2, spans[2], spans[3]))
        )

    def iota(shape, axis):
        return lax.broadcasted_iota(jnp.int32, shape, axis)

    enc_mask = spans_of(iota((ROWS, TOK), 0) >> 6) == (iota((ROWS, TOK), 1) >> 6)
    slots_t = iota((TOK, ROWS), 1) >> 6
    dec_mask = (spans_of(slots_t) == (iota((TOK, ROWS), 0) >> 6)) & (slots_t < counts[0])

    def softmax(scores, mask):
        scores = jnp.where(mask, scores * SCALE, NEG_LARGE)
        top = jnp.max(scores, axis=-1, keepdims=True)
        raised = jnp.where(mask, jnp.exp(scores - top), 0.0)
        return raised / jnp.sum(raised, axis=-1, keepdims=True)

    def head(i, second=False):
        start = i * HD + (HALF if second else 0)
        return slice(start, start + HD)

    def mine_head(i):
        return pl.ds(pl.multiple_of(g * HALF + i * HD, HD), HD)

    me8 = y * 2 + g
    for i in range(HEADS):
        probs = softmax(nt(qe[:, head(i)], skv[:, head(i)]), enc_mask)
        pe[i] = probs
        o = nn(probs.astype(BF), skv[:, head(i, True)])
        eb[me8, :, head(i)] = (neigh[:, mine_head(i)].astype(F32) + o).astype(BF)

    def ehalf(grp, rows):
        return lambda r, k: eb.at[mod4(y + r) * 2 + grp, pl.ds(k * rows, rows), :]

    def elow(r, grp):
        return eb.at[mod4(y + r) * 2 + grp, pl.ds(128, 128), :]

    e_slot = comm.alloc(4)

    def relay(i, r):
        comm.send(e_slot + i, elow(r, g), elow(r, g), partner)

    comm.send(e_slot, eb.at[me8], eb.at[me8], partner)
    ring_own, ring_other = Ring(comm, ehalf(g, 128), yp, ym), Ring(comm, ehalf(1 - g, 64), yp, ym)
    ring_own.start()
    slots[5].forward()
    slots[6].start()
    comm.recv(e_slot, eb.at[y * 2 + 1 - g], partner)
    ring_other.start()
    ring_own.forward()
    slots[5].rest()
    ring_own.near()
    relay(1, 1)
    relay(2, -1)
    slots[6].forward()
    slots[7].start()
    ring_other.forward()
    ring_own.far()
    relay(3, 2)
    slots[6].rest()
    ring_other.near()
    ring_other.far()
    slots[7].forward()
    for i, r in ((1, 1), (2, -1), (3, 2)):
        comm.recv(e_slot + i, elow(r, 1 - g), partner)

    def esum(i, carry):
        v = eb[i].astype(F32)
        return carry + jnp.sum(v * v, axis=1, keepdims=True)

    inv_enc = lax.rsqrt(lax.fori_loop(0, 8, esum, jnp.zeros((ROWS, 1), F32)) / FEATURES + EPSILON)

    for h in range(2):

        def norm_enc(i, carry, h=h):
            gain = gb[i, 0, 1:2, h * HALF : (h + 1) * HALF]
            en[i * 2 + h] = (eb[i * 2 + h].astype(F32) * inv_enc * gain).astype(BF)
            return carry

        lax.fori_loop(0, 4, norm_enc, 0)

    acc2[...] = jnp.zeros_like(acc2)

    def project_enc(i):
        shared(0, i)
        z = mod4(zh + ORDER[0][i])

        def step(k, carry):
            cols = pl.ds(pl.multiple_of((z % 2) * 256, 256), 256)
            acc2[...] += nn(en[k * 2 + z // 2, :, cols], w[0, k, z].reshape(256, COLS))
            return carry

        lax.fori_loop(0, 4, step, 0)

    for i in range(3):
        project_enc(i)
    slots[7].rest()
    project_enc(3)
    nkv[...] = acc2[...].astype(BF)

    mx_slot = comm.alloc(1)
    rowdot = jnp.zeros((ROWS, 1), F32)
    heads = range(HEADS)
    q = [dq[:, head(i)] for i in heads]
    k = [nkv[:, head(i)] for i in heads]
    v = [nkv[:, head(i, True)] for i in heads]
    ct = [cot[:, mine_head(i)] for i in heads]
    scores = [nt(q[i], k[i]) for i in heads]
    grad_probs = [nt(ct[i], v[i]) for i in heads]
    probs = [softmax(scores[i], dec_mask) for i in heads]
    rounded = [probs[i].astype(BF) for i in heads]
    grad_scores = [
        (probs[i] * (grad_probs[i] - jnp.sum(grad_probs[i] * probs[i], axis=-1, keepdims=True))).astype(BF)
        for i in heads
    ]
    grad_values = [tn(rounded[i], ct[i]) for i in heads]
    grad_keys = [tn(grad_scores[i], q[i]) * SCALE for i in heads]
    for i in heads:
        g2[:, head(i)] = grad_keys[i].astype(BF)
        g2[:, head(i, True)] = grad_values[i].astype(BF)
    for i in heads:
        mxs[:, head(i)] = nn(rounded[i], v[i]).astype(BF)
        rowdot = rowdot + jnp.sum(
            grad_keys[i] * k[i].astype(F32) + grad_values[i] * v[i].astype(F32), axis=1, keepdims=True
        )
    mx_copy = comm.copy(mx_slot, mxs, mxr, partner)

    rd[y] = as_row(rowdot)
    rd_base = comm.alloc(4)
    small_start(rd, rd_base)

    def back_enc(r, h):
        b = mod4(y + r) * 2 + h
        pb[b] = nt(g2[...], w[0, b // 2, pl.ds((b % 2) * 2, 2)].reshape(HALF, COLS)).astype(BF)

    LOW = ROWS // 2

    def part_of(r, h, low):
        return pb.at[mod4(y + r) * 2 + h, pl.ds(LOW if low else 0, LOW), :]

    def scatter_of(h, low, j):
        return Scatter(
            comm,
            lambda r: part_of(r, h, low),
            (rba.at[j, 0], rba.at[j, 1], rbb.at[j, 0], rbb.at[j, 1]),
            yp, ym, LOW,
        )

    away, home, low = scatter_of(1 - g, False, 0), scatter_of(g, False, 1), scatter_of(g, True, 2)
    low_slot = comm.alloc(4)

    def lower(i, r):
        comm.send(low_slot + i, part_of(r, 1 - g, True), lz.at[i], partner)

    def lower_add(i, r):
        comm.recv(low_slot + i, lz.at[i], partner)
        a = part_of(r, g, True)
        a[...] = (a[...].astype(F32) + lz[i].astype(F32)).astype(BF)

    back_enc(2, 1 - g)
    away.first()
    lower(0, 2)
    back_enc(1, 1 - g)
    lower(1, 1)
    back_enc(-1, 1 - g)
    lower(2, -1)
    away.second()
    back_enc(2, g)
    home.first()
    back_enc(0, 1 - g)
    lower(3, 0)
    back_enc(1, g)
    back_enc(-1, g)
    away.third()
    home.second()
    small_wait(rd, rd_base)
    rdp[0] = rd[0] + rd[1] + rd[2] + rd[3]
    comm.send(rd_base + 3, rdp.at[0], rdp.at[1], partner)
    back_enc(0, g)
    lower_add(0, 2)
    low.first()
    home.third()
    ysum[...] = away.total().astype(BF)
    r3_slot = comm.alloc(1)
    comm.send(r3_slot, ysum, r3, partner)
    lower_add(1, 1)
    lower_add(2, -1)
    low.second()
    low.third()

    @pl.when(g == 1)
    def _():
        mx_copy.start()

    comm.recv(rd_base + 3, rdp.at[1], partner)
    dot_all = as_col(rdp[0] + rdp[1])
    lower_add(3, 0)
    upper_in = home.total()
    comm.recv(r3_slot, r3, partner)
    grad_in = jnp.concatenate([upper_in + r3[...].astype(F32), low.total()], axis=0)
    grad_enc = (
        inv_enc * gb[y, 0, 1:2, mine] * grad_in
        - eb[me8].astype(F32) * (inv_enc * inv_enc * dot_all / FEATURES)
    ).astype(BF)

    rowdot1 = jnp.zeros((TOK, 1), F32)
    q = [qe[:, head(i)] for i in heads]
    k = [skv[:, head(i)] for i in heads]
    v = [skv[:, head(i, True)] for i in heads]
    go = [grad_enc[:, head(i)] for i in heads]
    probs = [pe[i] for i in heads]
    grad_probs = [nt(go[i], v[i]) for i in heads]
    grad_values = [tn(probs[i].astype(BF), go[i]) for i in heads]
    grad_scores = [
        (probs[i] * (grad_probs[i] - jnp.sum(grad_probs[i] * probs[i], axis=-1, keepdims=True))).astype(BF)
        for i in heads
    ]
    grad_keys = [tn(grad_scores[i], q[i]) * SCALE for i in heads]
    for i in heads:
        g1[:, head(i)] = grad_keys[i].astype(BF)
        g1[:, head(i, True)] = grad_values[i].astype(BF)
    for i in heads:
        rowdot1 = rowdot1 + jnp.sum(
            grad_keys[i] * k[i].astype(F32) + grad_values[i] * v[i].astype(F32), axis=1, keepdims=True
        )
    rd1[y] = as_row(rowdot1)
    rd1_base = comm.alloc(4)
    small_start(rd1, rd1_base)

    def back_state(r, h):
        b = mod4(y + r) * 2 + h
        pb1[b] = nt(g1[...], w[1, b // 2, pl.ds((b % 2) * 2, 2)].reshape(HALF, COLS)).astype(BF)

    def scatter_state(h):
        return Scatter(
            comm,
            lambda r: pb1.at[mod4(y + r) * 2 + h],
            (rca.at[h, 0], rca.at[h, 1], rcb.at[h, 0], rcb.at[h, 1]),
            yp, ym, TOK,
        )

    sc = [scatter_state(0), scatter_state(1)]
    for h in range(2):
        back_state(2, h)
        sc[h].first()
        back_state(1, h)
        back_state(-1, h)
        sc[h].second()
    sc[0].third()
    back_state(0, 0)
    back_state(0, 1)
    sc[1].third()
    small_wait(rd1, rd1_base)
    rdp1[0] = rd1[0] + rd1[1] + rd1[2] + rd1[3]
    comm.send(rd1_base + 3, rdp1.at[0], rdp1.at[1], partner)
    t3_slot = comm.alloc(2)
    t3_copies = [comm.copy(t3_slot + h, ysum1.at[h], t3.at[h], partner) for h in range(2)]
    for h in range(2):
        ysum1[h] = sc[h].total().astype(BF)

        @pl.when(g == 0)
        def _(h=h):
            t3_copies[h].start()

    comm.recv(rd1_base + 3, rdp1.at[1], partner)

    @pl.when(g == 0)
    def _():
        mx_copy.wait_recv()
        for h in range(2):
            heads_out = mxr if h == 1 else mxs
            cols = slice(h * HALF, (h + 1) * HALF)
            out[:, cols] = states[:, cols].astype(F32) + heads_out[...].astype(F32)
        for copy in t3_copies:
            copy.wait_send()

    @pl.when(g == 1)
    def _():
        dot_state = as_col(rdp1[0] + rdp1[1])
        factor = inv_state * inv_state * dot_state / FEATURES
        for h in range(2):
            t3_copies[h].wait_recv()
            cols = slice(h * HALF, (h + 1) * HALF)
            total = ysum1[h].astype(F32) + t3[h].astype(F32)
            out[:, cols] = (
                inv_state * gb[y, 1, 0:1, cols] * total - states[:, cols].astype(F32) * factor
            )
        mx_copy.wait_send()

    comm.drain()
    either(lambda grp: ([make().wait_send() for make in zsent[grp]], None)[1])


def per_device(states, neighbours, cotangent, span_of, counts, kv_weight, gains):
    wide = kv_weight.reshape(TOK, 2 * COLS)
    vmem, smem, hbm = (
        pl.BlockSpec(memory_space=m) for m in (pltpu.VMEM, pltpu.SMEM, pl.ANY)
    )

    def bf(*shape):
        return pltpu.VMEM(shape, BF)

    def f32(*shape):
        return pltpu.VMEM(shape, F32)

    scratch = [
        bf(2, 4, 4, 2, TOK, COLS),
        bf(TOK, COLS),
        bf(TOK, COLS),
        bf(ROWS, COLS),
        bf(TOK, COLS),
        bf(4, TOK, COLS),
        bf(4, TOK, COLS),
        f32(4, 2, 8, COLS),
        f32(4, 8, ROWS),
        bf(8, ROWS, HALF),
        bf(8, ROWS, HALF),
        f32(TOK, COLS),
        bf(TOK, COLS),
        bf(ROWS, HALF),
        f32(HEADS, ROWS, TOK),
        f32(ROWS, COLS),
        bf(ROWS, COLS),
        bf(TOK, HALF),
        bf(ROWS, COLS),
        bf(8, ROWS, HALF),
        bf(4, ROWS // 2, HALF),
        bf(3, 2, ROWS // 4, HALF),
        bf(3, 2, ROWS // 2, HALF),
        bf(ROWS // 2, HALF),
        bf(ROWS // 2, HALF),
        bf(TOK, COLS),
        bf(8, TOK, HALF),
        bf(2, 2, TOK // 2, HALF),
        bf(2, 2, TOK, HALF),
        bf(2, TOK, HALF),
        bf(2, TOK, HALF),
        f32(4, 8, ROWS),
        f32(2, 8, ROWS),
        f32(4, 8, TOK),
        f32(2, 8, TOK),
        bf(TOK, HALF),
        bf(TOK, HALF),
        pltpu.SemaphoreType.DMA((SEMS,)),
        pltpu.SemaphoreType.DMA((SEMS,)),
        pltpu.SemaphoreType.DMA((7,)),
    ]
    result = pl.pallas_call(
        kernel,
        out_shape=jax.ShapeDtypeStruct((TOK, COLS), F32),
        in_specs=[hbm, hbm, hbm, hbm, smem, smem, vmem],
        out_specs=vmem,
        scratch_shapes=scratch,
        compiler_params=pltpu.CompilerParams(
            collective_id=0, has_side_effects=True, vmem_limit_bytes=60 * 1024 * 1024
        ),
        name="spanned_attention",
    )(
        wide,
        states,
        neighbours.reshape(ROWS, COLS),
        cotangent,
        span_of,
        counts,
        gains.reshape(2, COLS),
    )
    return result[None]


def solution(mesh):
    return jax.shard_map(
        per_device,
        mesh=mesh,
        in_specs=(
            P("dp", "mp"),
            P("dp", None, "mp"),
            P("dp", "mp"),
            P("dp"),
            P("dp"),
            P("group", "dp", None, "mp"),
            P("group", None, "mp"),
        ),
        out_specs=P("group", "dp", "mp"),
        check_vma=False,
    )
```

```python
import functools

import jax
import jax.numpy as jnp
from jax import lax
from jax.experimental import pallas as pl
from jax.experimental.pallas import tpu as pltpu
from jax.sharding import PartitionSpec as P

HD = 128
FEATURES = 4096
CH = 64
EPSILON = 1e-05
NEG_LARGE = -1e30
TOK = 128
ROWS = 256
COLS = 1024
HALF = 512
HEADS = 4
SCALE = HD ** (-0.5)
BF = jnp.bfloat16
F32 = jnp.float32
SEMS = 320
AROWS = TOK
LOW = 96
LOW1 = 32
SPLIT = 64


def nt(a, b):
    return lax.dot_general(a, b, (((1,), (1,)), ((), ())), preferred_element_type=F32)


def nn(a, b):
    return lax.dot_general(a, b, (((1,), (0,)), ((), ())), preferred_element_type=F32)


def tn(a, b):
    return lax.dot_general(a, b, (((0,), (0,)), ((), ())), preferred_element_type=F32)


class Comm:
    def __init__(self, ssem, rsem):
        self.ssem, self.rsem = ssem, rsem
        self.used, self.sent = 0, []

    def alloc(self, count):
        base = self.used
        self.used += count
        assert self.used <= SEMS
        return base

    def copy(self, slot, src, dst, dev):
        return pltpu.make_async_remote_copy(
            src_ref=src,
            dst_ref=dst,
            send_sem=self.ssem.at[slot],
            recv_sem=self.rsem.at[slot],
            device_id=dev,
            device_id_type=pl.DeviceIdType.MESH,
        )

    def send(self, slot, src, dst, dev):
        copy = self.copy(slot, src, dst, dev)
        copy.start()
        self.sent.append(copy)

    def recv(self, slot, dst, dev):
        self.copy(slot, dst, dst, dev).wait_recv()

    def drain(self):
        for copy in self.sent:
            copy.wait_send()


class Ring:
    def __init__(self, comm, half, plus, minus):
        self.comm, self.half, self.plus, self.minus = comm, half, plus, minus
        self.base = comm.alloc(6)

    def start(self):
        for slot, k, dev in ((0, 0, self.plus), (2, 1, self.minus), (1, 1, self.plus), (3, 0, self.minus)):
            self.comm.send(self.base + slot, self.half(0, k), self.half(0, k), dev)

    def forward(self):
        self.comm.recv(self.base, self.half(-1, 0), self.minus)
        self.comm.send(self.base + 4, self.half(-1, 0), self.half(-1, 0), self.plus)
        self.comm.recv(self.base + 2, self.half(1, 1), self.plus)
        self.comm.send(self.base + 5, self.half(1, 1), self.half(1, 1), self.minus)

    def near(self):
        self.comm.recv(self.base + 1, self.half(-1, 1), self.minus)
        self.comm.recv(self.base + 3, self.half(1, 0), self.plus)

    def far(self):
        self.comm.recv(self.base + 4, self.half(2, 0), self.minus)
        self.comm.recv(self.base + 5, self.half(2, 1), self.plus)


class Scatter:
    def __init__(self, comm, part, bufs, plus, minus, rows):
        self.comm, self.part, self.plus, self.minus, self.n = comm, part, plus, minus, rows // 2
        self.from_minus, self.from_plus, self.last_minus, self.last_plus = bufs
        self.base = comm.alloc(6)

    def lo(self, ref):
        return ref.at[pl.ds(0, self.n), :]

    def hi(self, ref):
        return ref.at[pl.ds(self.n, self.n), :]

    def first(self):
        self.comm.send(self.base, self.lo(self.part(2)), self.from_minus, self.plus)
        self.comm.send(self.base + 1, self.hi(self.part(2)), self.from_plus, self.minus)

    def second(self):
        self.comm.send(self.base + 2, self.hi(self.part(1)), self.hi(self.last_minus), self.plus)
        self.comm.send(self.base + 3, self.lo(self.part(-1)), self.lo(self.last_plus), self.minus)

    def third(self):
        self.comm.recv(self.base, self.from_minus, self.minus)
        a = self.lo(self.part(1))
        a[...] = (a[...].astype(F32) + self.from_minus[...].astype(F32)).astype(BF)
        self.comm.send(self.base + 4, a, self.lo(self.last_minus), self.plus)
        self.comm.recv(self.base + 1, self.from_plus, self.plus)
        b = self.hi(self.part(-1))
        b[...] = (b[...].astype(F32) + self.from_plus[...].astype(F32)).astype(BF)
        self.comm.send(self.base + 5, b, self.hi(self.last_plus), self.minus)

    def total(self):
        self.comm.recv(self.base + 2, self.hi(self.last_minus), self.minus)
        self.comm.recv(self.base + 3, self.lo(self.last_plus), self.plus)
        self.comm.recv(self.base + 4, self.lo(self.last_minus), self.minus)
        self.comm.recv(self.base + 5, self.hi(self.last_plus), self.plus)
        return (
            self.part(0)[...].astype(F32)
            + self.last_minus[...].astype(F32)
            + self.last_plus[...].astype(F32)
        )


def as_row(col):
    return jnp.transpose(jnp.broadcast_to(col, (col.shape[0], 128)))[0:8, :]


def as_col(row):
    return jnp.transpose(jnp.broadcast_to(row[0:1, :], (128, row.shape[1])))[:, 0:1]


def kernel(
    wide, states_in, neigh_in, cot_in, span, counts, gains, out,
    w, theirs, states, neigh, cot, sx, xn, gb, ns, eb, en, acc1, skv, qe, pe, acc2, nkv, dq, g2, pb, lz, rba, rbb, r3, ysum,
    g1, pb1, lz1, rca, rcb, t3, ysum1, rd, rdp, rd1, rdp1, mxs, mxr,
    ssem, rsem, lsem,
):
    g = lax.axis_index("group")
    d = lax.axis_index("dp")
    y = lax.axis_index("mp")
    x, zh, c = d // 8, (d // 2) % 4, d % 2
    comm = Comm(ssem, rsem)

    def mod4(v):
        return (v + 4) % 4

    def at_x(r):
        return {"dp": mod4(x + r) * 8 + zh * 2 + c}

    def at_z(r):
        return {"dp": x * 8 + mod4(zh + r) * 2 + c}

    def at_y(r):
        return {"mp": mod4(y + r)}

    partner = {"group": 1 - g}
    sibling = {"dp": d + 1 - 2 * c}
    xp, xm, zp, zm, yp, ym, y2 = at_x(1), at_x(-1), at_z(1), at_z(-1), at_y(1), at_y(-1), at_y(2)

    across = {"group": 1 - g, "dp": x * 8 + mod4(zh + 2 * g - 1) * 2 + c}
    fetch = [
        pltpu.make_async_copy(src, dst, lsem.at[i])
        for i, (src, dst) in enumerate(((states_in, states), (neigh_in, neigh), (cot_in, cot)))
    ]
    local = []
    for i, (grp, dst) in enumerate(((g, w.at[g, x, zh, c]), (1 - g, theirs))):
        for pair in range(2):
            cols = pl.ds(pl.multiple_of(pair * COLS + grp * HALF, HALF), HALF)
            to = dst.at[:, pl.ds(pair * HALF, HALF)]
            local.append(pltpu.make_async_copy(wide.at[:, cols], to, lsem.at[3 + 2 * i + pair]))
            local[-1].start()
    for copy in fetch:
        copy.start()
    barrier = pltpu.get_barrier_semaphore()
    peers = (partner, sibling, xp, xm, zp, zm, yp, ym, y2, across)
    for dev in peers:
        pl.semaphore_signal(barrier, inc=1, device_id=dev, device_id_type=pl.DeviceIdType.MESH)
    for copy in fetch:
        copy.wait()
    nf = neigh[...].astype(F32)
    sq_rows = as_row(jnp.sum(nf * nf, axis=1, keepdims=True))
    sx[y] = states[...]
    even = lax.broadcasted_iota(jnp.int32, (8, COLS), 0) % 2 == 0
    gb[y, g] = jnp.where(even, gains[0:1, :], gains[1:2, :])
    for copy in local:
        copy.wait()
    pl.semaphore_wait(barrier, len(peers))

    ORDER = {1: (0, -1, 1, 2), 0: (0, 1, -1, 2)}
    PLAN = {
        1: [(1, 0), (0, 0), (1, 1), (1, 2), (1, 3), (0, 1), (0, 2), (0, 3)],
        0: [(0, 0), (1, 0), (1, 1), (1, 2), (1, 3), (0, 1), (0, 2), (0, 3)],
    }
    zbase = {m: comm.alloc(10) for m in (0, 1)}
    zsent = {0: [], 1: []}

    def whole(m, rx, rz, core):
        return w.at[m, mod4(x + rx), mod4(zh + rz), core]

    def main(m, rx, rz, core):
        return whole(m, rx, rz, core).at[pl.ds(0, AROWS), :]

    def main_half(m, rx, rz, k):
        rows = pl.ds(0, SPLIT) if k == 0 else pl.ds(SPLIT, AROWS - SPLIT)
        return whole(m, rx, rz, c).at[rows, :]

    def either(fn):
        for grp in (0, 1):
            pl.when(g == grp)(functools.partial(fn, grp))

    def zhalf(m, rz, k):
        return main_half(m, 0, rz, k)

    def zsend(grp, slot, ref, dev, src=None):
        def make():
            dst = ref()
            return comm.copy(slot, dst if src is None else src(), dst, dev)

        make().start()
        zsent[grp].append(make)

    def zpartner(grp):
        zsend(grp, zbase[grp] + 6, lambda: whole(grp, 0, 0, c), partner, lambda: theirs)

    def zout(grp):
        m, base = grp, zbase[grp]
        zsend(
            grp, base + 7, lambda: main(m, 0, 0, c), across, lambda: theirs.at[pl.ds(0, AROWS), :]
        )
        for slot, k, dev in ((0, 0, zp), (2, 1, zm), (1, 1, zp), (3, 0, zm)):
            zsend(grp, base + slot, lambda k=k: zhalf(m, 0, k), dev)

    def zarrive(grp, m, i):
        base, rz = zbase[m], ORDER[m][i]
        if grp == m:
            if i == 0:
                return
            if i == 1:
                comm.recv(base, zhalf(m, -1, 0), zm)
                zsend(grp, base + 4, lambda: zhalf(m, -1, 0), zp)
                comm.recv(base + 2, zhalf(m, 1, 1), zp)
                zsend(grp, base + 5, lambda: zhalf(m, 1, 1), zm)
            if rz == -1:
                comm.recv(base + 1, zhalf(m, -1, 1), zm)
            elif rz == 1:
                comm.recv(base + 3, zhalf(m, 1, 0), zp)
            else:
                comm.recv(base + 4, zhalf(m, 2, 0), zm)
                comm.recv(base + 5, zhalf(m, 2, 1), zp)
            return
        if i == 0:
            comm.recv(base + 6, whole(m, 0, 0, c), partner)
            if m == 1:
                zsend(grp, base + 8, lambda: main(m, 0, 0, c), zm)
        elif i == 1:
            if m == 0:
                zsend(grp, base + 8, lambda: main(m, 0, 0, c), zp)
            comm.recv(base + 7, main(m, 0, rz, c), across)
            zsend(grp, base + 9, lambda: main(m, 0, rz, c), zp if m == 1 else zm)
        else:
            comm.recv(base + 6 + i, main(m, 0, rz, c), zp)

    def plan(grp, s):
        m, i = PLAN[grp][s]
        return m, ORDER[m][i]

    class Slot:
        def __init__(self, s):
            (m0, r0), (m1, r1) = plan(0, s), plan(1, s)
            self.s, self.m, self.rz = s, m0 + (m1 - m0) * g, r0 + (r1 - r0) * g
            self.ring = Ring(comm, self.half, xp, xm)
            self.sib = comm.alloc(4)

        def half(self, r, k):
            return main_half(self.m, r, self.rz, k)

        def share(self, *rels):
            for rx in rels:
                block = main(self.m, rx, self.rz, c)
                comm.send(self.sib + rx % 4, block, block, sibling)

        def start(self):
            either(lambda grp: zarrive(grp, *PLAN[grp][self.s]))
            self.ring.start()
            self.share(0)

        def forward(self):
            self.ring.forward()

        def rest(self):
            self.ring.near()
            self.share(-1, 1)
            self.ring.far()
            self.share(2)

    slots = [Slot(s) for s in range(8)]
    sib_first = slots[0].sib
    sib_step = slots[1].sib - slots[0].sib

    def shared(m, i):
        s0, s1 = (PLAN[grp].index((m, i)) for grp in (0, 1))
        for rx in range(4):
            comm.recv(
                sib_first + (s0 + (s1 - s0) * g) * sib_step + rx,
                main(m, rx, ORDER[m][i], 1 - c),
                sibling,
            )

    either(zpartner)
    slots[0].start()

    def shalf(r, k):
        return sx.at[mod4(y + r), pl.ds(k * 64, 64), :]

    sring = Ring(comm, shalf, yp, ym)
    sring.start()
    gain_slot = comm.alloc(4)
    comm.send(gain_slot, gb.at[y, g], gb.at[y, g], partner)

    def small_start(buf, base):
        for i, (r, dev) in enumerate(((1, yp), (-1, ym), (2, y2))):
            comm.send(base + i, buf.at[y], buf.at[y], dev)

    def small_wait(buf, base):
        for i, (r, dev) in enumerate(((-1, ym), (1, yp), (2, y2))):
            comm.recv(base + i, buf.at[mod4(y + r)], dev)

    slots[0].forward()
    pl.when(g == 1)(lambda: zout(1))
    sring.forward()
    ns[y] = sq_rows
    ns_base = comm.alloc(3)
    small_start(ns, ns_base)
    comm.recv(gain_slot, gb.at[y, 1 - g], partner)
    small_start(gb, gain_slot + 1)
    slots[1].start()
    slots[0].rest()
    sring.near()
    sring.far()
    small_wait(ns, ns_base)
    small_wait(gb, gain_slot + 1)
    slots[1].forward()
    slots[2].start()

    mine = pl.ds(pl.multiple_of(g * HALF, HALF), HALF)
    sums = jnp.zeros((TOK, 1), F32)
    for i in range(4):
        v = sx[i].astype(F32)
        sums = sums + jnp.sum(v * v, axis=1, keepdims=True)
    inv_state = lax.rsqrt(sums / FEATURES + EPSILON)

    def norm_states(i, carry):
        xn[i] = (sx[i].astype(F32) * inv_state * gb[i, 1, 0:1, :]).astype(BF)
        return carry

    lax.fori_loop(0, 4, norm_states, 0)
    dq[...] = (states[:, mine].astype(F32) * inv_state * gb[y, 0, 0:1, mine]).astype(BF)
    inv_neigh = as_col(lax.rsqrt((ns[0] + ns[1] + ns[2] + ns[3]) / FEATURES + EPSILON))
    qe[...] = (neigh[:, mine].astype(F32) * inv_neigh * gb[y, 1, 1:2, mine]).astype(BF)

    def project_states(i):
        shared(1, i)
        z = mod4(zh + ORDER[1][i])

        def step(k, carry):
            part = nn(xn[k, :, pl.ds(pl.multiple_of(z * 256, 256), 256)], w[1, k, z].reshape(256, COLS))
            acc1[...] += part
            return carry

        lax.fori_loop(0, 4, step, 0)

    acc1[...] = jnp.zeros_like(acc1)
    slots[1].rest()
    slots[2].forward()
    slots[3].start()
    pl.when(g == 0)(lambda: zout(0))
    slots[2].rest()
    slots[3].forward()
    slots[4].start()
    slots[3].rest()
    slots[4].forward()
    slots[5].start()
    project_states(0)
    project_states(1)
    project_states(2)
    slots[4].rest()
    project_states(3)
    skv[...] = acc1[...].astype(BF)

    base_span = d * 2

    def spans_of(slot):
        spans = [span[i] - base_span for i in range(4)]
        return jnp.where(
            slot == 0, spans[0], jnp.where(slot == 1, spans[1], jnp.where(slot == 2, spans[2], spans[3]))
        )

    def iota(shape, axis):
        return lax.broadcasted_iota(jnp.int32, shape, axis)

    enc_mask = spans_of(iota((ROWS, TOK), 0) >> 6) == (iota((ROWS, TOK), 1) >> 6)
    slots_t = iota((TOK, ROWS), 1) >> 6
    dec_mask = (spans_of(slots_t) == (iota((TOK, ROWS), 0) >> 6)) & (slots_t < counts[0])

    def softmax(scores, mask):
        scores = jnp.where(mask, scores * SCALE, NEG_LARGE)
        top = jnp.max(scores, axis=-1, keepdims=True)
        raised = jnp.where(mask, jnp.exp(scores - top), 0.0)
        return raised / jnp.sum(raised, axis=-1, keepdims=True)

    def head(i, second=False):
        start = i * HD + (HALF if second else 0)
        return slice(start, start + HD)

    def mine_head(i):
        return pl.ds(pl.multiple_of(g * HALF + i * HD, HD), HD)

    me8 = y * 2 + g
    for i in range(HEADS):
        probs = softmax(nt(qe[:, head(i)], skv[:, head(i)]), enc_mask)
        pe[i] = probs
        o = nn(probs.astype(BF), skv[:, head(i, True)])
        eb[me8, :, head(i)] = (neigh[:, mine_head(i)].astype(F32) + o).astype(BF)

    def ehalf(grp, rows):
        return lambda r, k: eb.at[mod4(y + r) * 2 + grp, pl.ds(k * rows, rows), :]

    def elow(r, grp):
        return eb.at[mod4(y + r) * 2 + grp, pl.ds(128, 128), :]

    e_slot = comm.alloc(4)

    def relay(i, r):
        comm.send(e_slot + i, elow(r, g), elow(r, g), partner)

    comm.send(e_slot, eb.at[me8], eb.at[me8], partner)
    ring_own, ring_other = Ring(comm, ehalf(g, 128), yp, ym), Ring(comm, ehalf(1 - g, 64), yp, ym)
    ring_own.start()
    slots[5].forward()
    slots[6].start()
    ring_own.forward()
    slots[5].rest()
    comm.recv(e_slot, eb.at[y * 2 + 1 - g], partner)
    ring_other.start()
    ring_own.near()
    relay(1, 1)
    relay(2, -1)
    slots[6].forward()
    slots[7].start()
    ring_own.far()
    relay(3, 2)

    def squares(first):
        def add(i, carry):
            v = eb[i * 2 + first].astype(F32)
            return carry + jnp.sum(v * v, axis=1, keepdims=True)

        return lax.fori_loop(0, 4, add, jnp.zeros((ROWS, 1), F32))

    enc_sum = squares(g)
    ring_other.forward()
    slots[6].rest()
    ring_other.near()
    ring_other.far()
    slots[7].forward()
    for i, r in ((1, 1), (2, -1), (3, 2)):
        comm.recv(e_slot + i, elow(r, 1 - g), partner)
    inv_enc = lax.rsqrt((enc_sum + squares(1 - g)) / FEATURES + EPSILON)

    for h in range(2):

        def norm_enc(i, carry, h=h):
            gain = gb[i, 0, 1:2, h * HALF : (h + 1) * HALF]
            en[i * 2 + h] = (eb[i * 2 + h].astype(F32) * inv_enc * gain).astype(BF)
            return carry

        lax.fori_loop(0, 4, norm_enc, 0)

    acc2[...] = jnp.zeros_like(acc2)

    def project_enc(i):
        shared(0, i)
        z = mod4(zh + ORDER[0][i])

        def step(k, carry):
            cols = pl.ds(pl.multiple_of((z % 2) * 256, 256), 256)
            acc2[...] += nn(en[k * 2 + z // 2, :, cols], w[0, k, z].reshape(256, COLS))
            return carry

        lax.fori_loop(0, 4, step, 0)

    for i in range(3):
        project_enc(i)
    slots[7].rest()
    project_enc(3)
    nkv[...] = acc2[...].astype(BF)

    mx_slot = comm.alloc(1)
    rowdot = jnp.zeros((ROWS, 1), F32)
    heads = range(HEADS)
    q = [dq[:, head(i)] for i in heads]
    k = [nkv[:, head(i)] for i in heads]
    v = [nkv[:, head(i, True)] for i in heads]
    ct = [cot[:, mine_head(i)] for i in heads]
    scores = [nt(q[i], k[i]) for i in heads]
    grad_probs = [nt(ct[i], v[i]) for i in heads]
    probs = [softmax(scores[i], dec_mask) for i in heads]
    rounded = [probs[i].astype(BF) for i in heads]
    grad_scores = [
        (probs[i] * (grad_probs[i] - jnp.sum(grad_probs[i] * probs[i], axis=-1, keepdims=True))).astype(BF)
        for i in heads
    ]
    grad_values = [tn(rounded[i], ct[i]) for i in heads]
    grad_keys = [tn(grad_scores[i], q[i]) * SCALE for i in heads]
    for i in heads:
        g2[:, head(i)] = grad_keys[i].astype(BF)
        g2[:, head(i, True)] = grad_values[i].astype(BF)
    for i in heads:
        mxs[:, head(i)] = nn(rounded[i], v[i]).astype(BF)
        rowdot = rowdot + jnp.sum(
            grad_keys[i] * k[i].astype(F32) + grad_values[i] * v[i].astype(F32), axis=1, keepdims=True
        )
    mx_copy = comm.copy(mx_slot, mxs, mxr, partner)

    rd[y] = as_row(rowdot)
    rd_base = comm.alloc(4)
    small_start(rd, rd_base)

    def back_enc(r, h):
        b = mod4(y + r) * 2 + h
        pb[b] = nt(g2[...], w[0, b // 2, pl.ds((b % 2) * 2, 2)].reshape(HALF, COLS)).astype(BF)

    def rows_of(low):
        return pl.ds(ROWS - LOW, LOW) if low else pl.ds(0, ROWS - LOW)

    def part_of(r, h, low):
        return pb.at[mod4(y + r) * 2 + h, rows_of(low), :]

    def scatter_of(h, low, j):
        n = LOW if low else ROWS - LOW
        short, whole_rows = pl.ds(0, n // 2), pl.ds(0, n)
        bufs = [rba.at[j, k, short, :] for k in (0, 1)] + [rbb.at[j, k, whole_rows, :] for k in (0, 1)]
        return Scatter(comm, lambda r: part_of(r, h, low), bufs, yp, ym, n)

    away, home, low = scatter_of(1 - g, False, 0), scatter_of(g, False, 1), scatter_of(g, True, 2)
    low_slot = comm.alloc(4)

    def lower(i, r):
        comm.send(low_slot + i, part_of(r, 1 - g, True), lz.at[i], partner)

    def lower_add(i, r):
        comm.recv(low_slot + i, lz.at[i], partner)
        a = part_of(r, g, True)
        a[...] = (a[...].astype(F32) + lz[i].astype(F32)).astype(BF)

    back_enc(2, 1 - g)
    away.first()
    lower(0, 2)
    back_enc(1, 1 - g)
    lower(1, 1)
    back_enc(-1, 1 - g)
    lower(2, -1)
    away.second()
    back_enc(2, g)
    home.first()
    back_enc(0, 1 - g)
    lower(3, 0)
    back_enc(1, g)
    back_enc(-1, g)
    away.third()
    home.second()
    small_wait(rd, rd_base)
    rdp[0] = rd[0] + rd[1] + rd[2] + rd[3]
    comm.send(rd_base + 3, rdp.at[0], rdp.at[1], partner)
    back_enc(0, g)
    lower_add(0, 2)
    low.first()
    home.third()
    ysum[...] = away.total().astype(BF)
    r3_slot = comm.alloc(1)
    comm.send(r3_slot, ysum, r3, partner)
    lower_add(1, 1)
    lower_add(2, -1)
    low.second()
    low.third()

    @pl.when(g == 1)
    def _():
        mx_copy.start()

    comm.recv(rd_base + 3, rdp.at[1], partner)
    dot_all = as_col(rdp[0] + rdp[1])
    lower_add(3, 0)
    upper_in = home.total()
    comm.recv(r3_slot, r3, partner)
    grad_in = jnp.concatenate([upper_in + r3[...].astype(F32), low.total()], axis=0)
    grad_enc = (
        inv_enc * gb[y, 0, 1:2, mine] * grad_in
        - eb[me8].astype(F32) * (inv_enc * inv_enc * dot_all / FEATURES)
    ).astype(BF)

    rowdot1 = jnp.zeros((TOK, 1), F32)
    q = [qe[:, head(i)] for i in heads]
    k = [skv[:, head(i)] for i in heads]
    v = [skv[:, head(i, True)] for i in heads]
    go = [grad_enc[:, head(i)] for i in heads]
    probs = [pe[i] for i in heads]
    grad_probs = [nt(go[i], v[i]) for i in heads]
    grad_values = [tn(probs[i].astype(BF), go[i]) for i in heads]
    grad_scores = [
        (probs[i] * (grad_probs[i] - jnp.sum(grad_probs[i] * probs[i], axis=-1, keepdims=True))).astype(BF)
        for i in heads
    ]
    grad_keys = [tn(grad_scores[i], q[i]) * SCALE for i in heads]
    for i in heads:
        g1[:, head(i)] = grad_keys[i].astype(BF)
        g1[:, head(i, True)] = grad_values[i].astype(BF)
    for i in heads:
        rowdot1 = rowdot1 + jnp.sum(
            grad_keys[i] * k[i].astype(F32) + grad_values[i] * v[i].astype(F32), axis=1, keepdims=True
        )
    rd1[y] = as_row(rowdot1)
    rd1_base = comm.alloc(4)
    small_start(rd1, rd1_base)

    def back_state(r, h):
        b = mod4(y + r) * 2 + h
        pb1[b] = nt(g1[...], w[1, b // 2, pl.ds((b % 2) * 2, 2)].reshape(HALF, COLS)).astype(BF)

    def token_part(r, h, low):
        rows = pl.ds(TOK - LOW1, LOW1) if low else pl.ds(0, TOK - LOW1)
        return pb1.at[mod4(y + r) * 2 + h, rows, :]

    def scatter_state(h, low):
        n, j = (LOW1 if low else TOK - LOW1), h * 2 + low
        short, whole_rows = pl.ds(0, n // 2), pl.ds(0, n)
        bufs = [rca.at[j, k, short, :] for k in (0, 1)] + [rcb.at[j, k, whole_rows, :] for k in (0, 1)]
        return Scatter(comm, lambda r: token_part(r, h, low), bufs, yp, ym, n)

    ups = [scatter_state(h, False) for h in range(2)]
    lows = [scatter_state(h, True) for h in range(2)]
    raw_slot = comm.alloc(8)
    raw = {}

    def raw_send(r, h):
        i = h * 4 + r % 4
        raw[r, h] = comm.copy(raw_slot + i, token_part(r, h, True), lz1.at[i], partner)
        pl.when(g == 0)(lambda: raw[r, h].start())

    def raw_add(*pairs):
        @pl.when(g == 1)
        def _():
            for r, h in pairs:
                raw[r, h].wait_recv()
                a = token_part(r, h, True)
                a[...] = (a[...].astype(F32) + lz1[h * 4 + r % 4].astype(F32)).astype(BF)

    for h in range(2):
        back_state(2, h)
        ups[h].first()
        raw_send(2, h)
        back_state(1, h)
        back_state(-1, h)
        ups[h].second()
        raw_send(1, h)
        raw_send(-1, h)
    for h in range(2):
        back_state(0, h)
        raw_send(0, h)
    ups[0].third()
    raw_add((2, 0), (2, 1))
    lows[0].first()
    lows[1].first()
    ups[1].third()
    small_wait(rd1, rd1_base)
    rdp1[0] = rd1[0] + rd1[1] + rd1[2] + rd1[3]
    comm.send(rd1_base + 3, rdp1.at[0], rdp1.at[1], partner)
    raw_add((1, 0), (-1, 0), (1, 1), (-1, 1))
    for h in range(2):
        lows[h].second()
    t3_slot = comm.alloc(2)
    t3_copies = [comm.copy(t3_slot + h, ysum1.at[h], t3.at[h], partner) for h in range(2)]
    for h in range(2):
        ysum1[h] = ups[h].total().astype(BF)

        @pl.when(g == 0)
        def _(h=h):
            t3_copies[h].start()
            for r in (1, -1):
                raw[r, h].wait_send()

        lows[h].third()

    raw_add((0, 0), (0, 1))
    low_sums = [lows[h].total() for h in range(2)]
    comm.recv(rd1_base + 3, rdp1.at[1], partner)

    @pl.when(g == 0)
    def _():
        mx_copy.wait_recv()
        for h in range(2):
            heads_out = mxr if h == 1 else mxs
            cols = slice(h * HALF, (h + 1) * HALF)
            out[:, cols] = states[:, cols].astype(F32) + heads_out[...].astype(F32)
        for copy in (*t3_copies, *(raw[r, h] for h in range(2) for r in (2, 0))):
            copy.wait_send()

    @pl.when(g == 1)
    def _():
        dot_state = as_col(rdp1[0] + rdp1[1])
        factor = inv_state * inv_state * dot_state / FEATURES
        for h in range(2):
            t3_copies[h].wait_recv()
            cols = slice(h * HALF, (h + 1) * HALF)
            upper = ysum1[h].astype(F32) + t3[h].astype(F32)
            total = jnp.concatenate([upper, low_sums[h]], axis=0)
            out[:, cols] = (
                inv_state * gb[y, 1, 0:1, cols] * total - states[:, cols].astype(F32) * factor
            )
        mx_copy.wait_send()

    comm.drain()
    either(lambda grp: ([make().wait_send() for make in zsent[grp]], None)[1])


def per_device(states, neighbours, cotangent, span_of, counts, kv_weight, gains):
    wide = kv_weight.reshape(TOK, 2 * COLS)
    vmem, smem, hbm = (
        pl.BlockSpec(memory_space=m) for m in (pltpu.VMEM, pltpu.SMEM, pl.ANY)
    )

    def bf(*shape):
        return pltpu.VMEM(shape, BF)

    def f32(*shape):
        return pltpu.VMEM(shape, F32)

    scratch = [
        bf(2, 4, 4, 2, TOK, COLS),
        bf(TOK, COLS),
        bf(TOK, COLS),
        bf(ROWS, COLS),
        bf(TOK, COLS),
        bf(4, TOK, COLS),
        bf(4, TOK, COLS),
        f32(4, 2, 8, COLS),
        f32(4, 8, ROWS),
        bf(8, ROWS, HALF),
        bf(8, ROWS, HALF),
        f32(TOK, COLS),
        bf(TOK, COLS),
        bf(ROWS, HALF),
        f32(HEADS, ROWS, TOK),
        f32(ROWS, COLS),
        bf(ROWS, COLS),
        bf(TOK, HALF),
        bf(ROWS, COLS),
        bf(8, ROWS, HALF),
        bf(4, LOW, HALF),
        bf(3, 2, (ROWS - LOW) // 2, HALF),
        bf(3, 2, ROWS - LOW, HALF),
        bf(ROWS - LOW, HALF),
        bf(ROWS - LOW, HALF),
        bf(TOK, COLS),
        bf(8, TOK, HALF),
        bf(8, LOW1, HALF),
        bf(4, 2, (TOK - LOW1) // 2, HALF),
        bf(4, 2, TOK - LOW1, HALF),
        bf(2, TOK - LOW1, HALF),
        bf(2, TOK - LOW1, HALF),
        f32(4, 8, ROWS),
        f32(2, 8, ROWS),
        f32(4, 8, TOK),
        f32(2, 8, TOK),
        bf(TOK, HALF),
        bf(TOK, HALF),
        pltpu.SemaphoreType.DMA((SEMS,)),
        pltpu.SemaphoreType.DMA((SEMS,)),
        pltpu.SemaphoreType.DMA((7,)),
    ]
    result = pl.pallas_call(
        kernel,
        out_shape=jax.ShapeDtypeStruct((TOK, COLS), F32),
        in_specs=[hbm, hbm, hbm, hbm, smem, smem, vmem],
        out_specs=vmem,
        scratch_shapes=scratch,
        compiler_params=pltpu.CompilerParams(
            collective_id=0, has_side_effects=True, vmem_limit_bytes=60 * 1024 * 1024
        ),
        name="spanned_attention",
    )(
        wide,
        states,
        neighbours.reshape(ROWS, COLS),
        cotangent,
        span_of,
        counts,
        gains.reshape(2, COLS),
    )
    return result[None]


def solution(mesh):
    return jax.shard_map(
        per_device,
        mesh=mesh,
        in_specs=(
            P("dp", "mp"),
            P("dp", None, "mp"),
            P("dp", "mp"),
            P("dp"),
            P("dp"),
            P("group", "dp", None, "mp"),
            P("group", None, "mp"),
        ),
        out_specs=P("group", "dp", "mp"),
        check_vma=False,
    )
```

```python
import functools

import jax
import jax.numpy as jnp
from jax import lax
from jax.experimental import pallas as pl
from jax.experimental.pallas import tpu as pltpu
from jax.sharding import PartitionSpec as P

HD = 128
FEATURES = 4096
CH = 64
EPSILON = 1e-05
NEG_LARGE = -1e30
TOK = 128
ROWS = 256
COLS = 1024
HALF = 512
HEADS = 4
SCALE = HD ** (-0.5)
BF = jnp.bfloat16
F32 = jnp.float32
SEMS = 320
AROWS = TOK
FAR_BY_Z = (4,)
UP = 160
LOW = 128
LOW1 = 32
SPLIT = 64


def nt(a, b):
    return lax.dot_general(a, b, (((1,), (1,)), ((), ())), preferred_element_type=F32)


def nn(a, b):
    return lax.dot_general(a, b, (((1,), (0,)), ((), ())), preferred_element_type=F32)


def tn(a, b):
    return lax.dot_general(a, b, (((0,), (0,)), ((), ())), preferred_element_type=F32)


class Comm:
    def __init__(self, ssem, rsem):
        self.ssem, self.rsem = ssem, rsem
        self.used, self.sent = 0, []

    def alloc(self, count):
        base = self.used
        self.used += count
        assert self.used <= SEMS
        return base

    def copy(self, slot, src, dst, dev):
        return pltpu.make_async_remote_copy(
            src_ref=src,
            dst_ref=dst,
            send_sem=self.ssem.at[slot],
            recv_sem=self.rsem.at[slot],
            device_id=dev,
            device_id_type=pl.DeviceIdType.MESH,
        )

    def send(self, slot, src, dst, dev):
        copy = self.copy(slot, src, dst, dev)
        copy.start()
        self.sent.append(copy)

    def recv(self, slot, dst, dev):
        self.copy(slot, dst, dst, dev).wait_recv()

    def drain(self):
        for copy in self.sent:
            copy.wait_send()


class Ring:
    def __init__(self, comm, half, plus, minus):
        self.comm, self.half, self.plus, self.minus = comm, half, plus, minus
        self.base = comm.alloc(6)

    def start(self):
        for slot, k, dev in ((0, 0, self.plus), (2, 1, self.minus), (1, 1, self.plus), (3, 0, self.minus)):
            self.comm.send(self.base + slot, self.half(0, k), self.half(0, k), dev)

    def forward(self):
        self.comm.recv(self.base, self.half(-1, 0), self.minus)
        self.comm.send(self.base + 4, self.half(-1, 0), self.half(-1, 0), self.plus)
        self.comm.recv(self.base + 2, self.half(1, 1), self.plus)
        self.comm.send(self.base + 5, self.half(1, 1), self.half(1, 1), self.minus)

    def near(self):
        self.comm.recv(self.base + 1, self.half(-1, 1), self.minus)
        self.comm.recv(self.base + 3, self.half(1, 0), self.plus)

    def far(self):
        self.comm.recv(self.base + 4, self.half(2, 0), self.minus)
        self.comm.recv(self.base + 5, self.half(2, 1), self.plus)


class Scatter:
    def __init__(self, comm, part, bufs, plus, minus, rows):
        self.comm, self.part, self.plus, self.minus, self.n = comm, part, plus, minus, rows // 2
        self.from_minus, self.from_plus, self.last_minus, self.last_plus = bufs
        self.base = comm.alloc(6)

    def lo(self, ref):
        return ref.at[pl.ds(0, self.n), :]

    def hi(self, ref):
        return ref.at[pl.ds(self.n, self.n), :]

    def first(self):
        self.comm.send(self.base, self.lo(self.part(2)), self.from_minus, self.plus)
        self.comm.send(self.base + 1, self.hi(self.part(2)), self.from_plus, self.minus)

    def second(self):
        self.comm.send(self.base + 2, self.hi(self.part(1)), self.hi(self.last_minus), self.plus)
        self.comm.send(self.base + 3, self.lo(self.part(-1)), self.lo(self.last_plus), self.minus)

    def third(self):
        self.comm.recv(self.base, self.from_minus, self.minus)
        a = self.lo(self.part(1))
        a[...] = (a[...].astype(F32) + self.from_minus[...].astype(F32)).astype(BF)
        self.comm.send(self.base + 4, a, self.lo(self.last_minus), self.plus)
        self.comm.recv(self.base + 1, self.from_plus, self.plus)
        b = self.hi(self.part(-1))
        b[...] = (b[...].astype(F32) + self.from_plus[...].astype(F32)).astype(BF)
        self.comm.send(self.base + 5, b, self.hi(self.last_plus), self.minus)

    def total(self):
        self.comm.recv(self.base + 2, self.hi(self.last_minus), self.minus)
        self.comm.recv(self.base + 3, self.lo(self.last_plus), self.plus)
        self.comm.recv(self.base + 4, self.lo(self.last_minus), self.minus)
        self.comm.recv(self.base + 5, self.hi(self.last_plus), self.plus)
        return (
            self.part(0)[...].astype(F32)
            + self.last_minus[...].astype(F32)
            + self.last_plus[...].astype(F32)
        )


def as_row(col):
    return jnp.transpose(jnp.broadcast_to(col, (col.shape[0], 128)))[0:8, :]


def as_col(row):
    return jnp.transpose(jnp.broadcast_to(row[0:1, :], (128, row.shape[1])))[:, 0:1]


def kernel(
    wide, states_in, neigh_in, cot_in, span, counts, gains, out,
    w, theirs, states, neigh, cot, sx, xn, gb, ns, eb, en, acc1, skv, qe, pe, acc2, nkv, dq, g2, pb, lz, rba, rbb, r3, ysum,
    g1, pb1, lz1, rca, rcb, t3, ysum1, rd, rdp, rd1, rdp1, mxs, mxr,
    ssem, rsem, lsem,
):
    g = lax.axis_index("group")
    d = lax.axis_index("dp")
    y = lax.axis_index("mp")
    x, zh, c = d // 8, (d // 2) % 4, d % 2
    comm = Comm(ssem, rsem)

    def mod4(v):
        return (v + 4) % 4

    def at_x(r):
        return {"dp": mod4(x + r) * 8 + zh * 2 + c}

    def at_z(r):
        return {"dp": x * 8 + mod4(zh + r) * 2 + c}

    def at_y(r):
        return {"mp": mod4(y + r)}

    partner = {"group": 1 - g}
    sibling = {"dp": d + 1 - 2 * c}
    xp, xm, zp, zm, yp, ym, y2 = at_x(1), at_x(-1), at_z(1), at_z(-1), at_y(1), at_y(-1), at_y(2)

    across = {"group": 1 - g, "dp": x * 8 + mod4(zh + 2 * g - 1) * 2 + c}
    fetch = [
        pltpu.make_async_copy(src, dst, lsem.at[i])
        for i, (src, dst) in enumerate(((states_in, states), (neigh_in, neigh), (cot_in, cot)))
    ]
    local = []
    for i, (grp, dst) in enumerate(((g, w.at[g, x, zh, c]), (1 - g, theirs))):
        for pair in range(2):
            cols = pl.ds(pl.multiple_of(pair * COLS + grp * HALF, HALF), HALF)
            to = dst.at[:, pl.ds(pair * HALF, HALF)]
            local.append(pltpu.make_async_copy(wide.at[:, cols], to, lsem.at[3 + 2 * i + pair]))
            local[-1].start()
    for copy in fetch:
        copy.start()
    barrier = pltpu.get_barrier_semaphore()
    peers = (partner, sibling, xp, xm, zp, zm, yp, ym, y2, across)
    for dev in peers:
        pl.semaphore_signal(barrier, inc=1, device_id=dev, device_id_type=pl.DeviceIdType.MESH)
    for copy in fetch:
        copy.wait()
    nf = neigh[...].astype(F32)
    sq_rows = as_row(jnp.sum(nf * nf, axis=1, keepdims=True))
    sx[y] = states[...]
    even = lax.broadcasted_iota(jnp.int32, (8, COLS), 0) % 2 == 0
    gb[y, g] = jnp.where(even, gains[0:1, :], gains[1:2, :])
    for copy in local:
        copy.wait()
    pl.semaphore_wait(barrier, len(peers))

    ORDER = {1: (0, -1, 1, 2), 0: (0, 1, -1, 2)}
    PLAN = {
        1: [(1, 0), (0, 0), (1, 1), (1, 2), (1, 3), (0, 1), (0, 2), (0, 3)],
        0: [(0, 0), (1, 0), (1, 1), (1, 2), (1, 3), (0, 1), (0, 2), (0, 3)],
    }
    zbase = {m: comm.alloc(10) for m in (0, 1)}
    zsent = {0: [], 1: []}

    def whole(m, rx, rz, core):
        return w.at[m, mod4(x + rx), mod4(zh + rz), core]

    def main(m, rx, rz, core):
        return whole(m, rx, rz, core).at[pl.ds(0, AROWS), :]

    def main_half(m, rx, rz, k):
        rows = pl.ds(0, SPLIT) if k == 0 else pl.ds(SPLIT, AROWS - SPLIT)
        return whole(m, rx, rz, c).at[rows, :]

    def either(fn):
        for grp in (0, 1):
            pl.when(g == grp)(functools.partial(fn, grp))

    def zhalf(m, rz, k):
        return main_half(m, 0, rz, k)

    def zsend(grp, slot, ref, dev, src=None):
        def make():
            dst = ref()
            return comm.copy(slot, dst if src is None else src(), dst, dev)

        make().start()
        zsent[grp].append(make)

    def zpartner(grp):
        zsend(grp, zbase[grp] + 6, lambda: whole(grp, 0, 0, c), partner, lambda: theirs)

    def zout(grp):
        m, base = grp, zbase[grp]
        zsend(
            grp, base + 7, lambda: main(m, 0, 0, c), across, lambda: theirs.at[pl.ds(0, AROWS), :]
        )
        for slot, k, dev in ((0, 0, zp), (2, 1, zm), (1, 1, zp), (3, 0, zm)):
            zsend(grp, base + slot, lambda k=k: zhalf(m, 0, k), dev)

    def zarrive(grp, m, i):
        base, rz = zbase[m], ORDER[m][i]
        if grp == m:
            if i == 0:
                return
            if i == 1:
                comm.recv(base, zhalf(m, -1, 0), zm)
                zsend(grp, base + 4, lambda: zhalf(m, -1, 0), zp)
                comm.recv(base + 2, zhalf(m, 1, 1), zp)
                zsend(grp, base + 5, lambda: zhalf(m, 1, 1), zm)
            if rz == -1:
                comm.recv(base + 1, zhalf(m, -1, 1), zm)
            elif rz == 1:
                comm.recv(base + 3, zhalf(m, 1, 0), zp)
            else:
                comm.recv(base + 4, zhalf(m, 2, 0), zm)
                comm.recv(base + 5, zhalf(m, 2, 1), zp)
            return
        if i == 0:
            comm.recv(base + 6, whole(m, 0, 0, c), partner)
            if m == 1:
                zsend(grp, base + 8, lambda: main(m, 0, 0, c), zm)
        elif i == 1:
            if m == 0:
                zsend(grp, base + 8, lambda: main(m, 0, 0, c), zp)
            comm.recv(base + 7, main(m, 0, rz, c), across)
            zsend(grp, base + 9, lambda: main(m, 0, rz, c), zp if m == 1 else zm)
        else:
            comm.recv(base + 6 + i, main(m, 0, rz, c), zp)

    def plan(grp, s):
        m, i = PLAN[grp][s]
        return m, ORDER[m][i]

    class Slot:
        def __init__(self, s):
            (m0, r0), (m1, r1) = plan(0, s), plan(1, s)
            self.m_, self.arrival = PLAN[0][s]
            self.s, self.m, self.rz = s, m0 + (m1 - m0) * g, r0 + (r1 - r0) * g
            self.ring = Ring(comm, self.half, xp, xm)
            self.sib = comm.alloc(4)
            self.far = comm.alloc(2)

        def half(self, r, k):
            return main_half(self.m, r, self.rz, k)

        def share(self, *rels):
            for rx in rels:
                block = main(self.m, rx, self.rz, c)
                comm.send(self.sib + rx % 4, block, block, sibling)

        def start(self):
            either(lambda grp: zarrive(grp, *PLAN[grp][self.s]))
            self.ring.start()
            self.share(0)

        def forward(self):
            if self.s not in FAR_BY_Z:
                self.ring.forward()

        def rest(self):
            if self.s in FAR_BY_Z:
                comm.recv(self.ring.base, self.half(-1, 0), xm)
                comm.recv(self.ring.base + 2, self.half(1, 1), xp)
            self.ring.near()
            self.share(-1, 1)
            if self.s in FAR_BY_Z:
                comm.recv(self.far, self.half(2, 0), zm)
                comm.recv(self.far + 1, self.half(2, 1), zp)
            else:
                self.ring.far()
            self.share(2)

        def pass_far(self, to):
            if to.s in FAR_BY_Z:
                k, dev = (0, zp) if ORDER[to.m_][self.arrival] == -1 else (1, zm)
                ref = self.half(2, k)
                comm.send(to.far + k, ref, ref, dev)

    slots = [Slot(s) for s in range(8)]
    sib_first = slots[0].sib
    sib_step = slots[1].sib - slots[0].sib

    def shared(m, i):
        s0, s1 = (PLAN[grp].index((m, i)) for grp in (0, 1))
        for rx in range(4):
            comm.recv(
                sib_first + (s0 + (s1 - s0) * g) * sib_step + rx,
                main(m, rx, ORDER[m][i], 1 - c),
                sibling,
            )

    either(zpartner)
    slots[0].start()

    def shalf(r, k):
        return sx.at[mod4(y + r), pl.ds(k * 64, 64), :]

    sring = Ring(comm, shalf, yp, ym)
    sring.start()
    gain_slot = comm.alloc(4)
    comm.send(gain_slot, gb.at[y, g], gb.at[y, g], partner)

    def small_start(buf, base):
        for i, (r, dev) in enumerate(((1, yp), (-1, ym), (2, y2))):
            comm.send(base + i, buf.at[y], buf.at[y], dev)

    def small_wait(buf, base):
        for i, (r, dev) in enumerate(((-1, ym), (1, yp), (2, y2))):
            comm.recv(base + i, buf.at[mod4(y + r)], dev)

    slots[0].forward()
    pl.when(g == 1)(lambda: zout(1))
    sring.forward()
    ns[y] = sq_rows
    ns_base = comm.alloc(3)
    small_start(ns, ns_base)
    comm.recv(gain_slot, gb.at[y, 1 - g], partner)
    small_start(gb, gain_slot + 1)
    slots[1].start()
    slots[0].rest()
    sring.near()
    sring.far()
    small_wait(ns, ns_base)
    small_wait(gb, gain_slot + 1)
    slots[1].forward()
    slots[2].start()

    mine = pl.ds(pl.multiple_of(g * HALF, HALF), HALF)
    sums = jnp.zeros((TOK, 1), F32)
    for i in range(4):
        v = sx[i].astype(F32)
        sums = sums + jnp.sum(v * v, axis=1, keepdims=True)
    inv_state = lax.rsqrt(sums / FEATURES + EPSILON)

    def norm_states(i, carry):
        xn[i] = (sx[i].astype(F32) * inv_state * gb[i, 1, 0:1, :]).astype(BF)
        return carry

    lax.fori_loop(0, 4, norm_states, 0)
    dq[...] = (states[:, mine].astype(F32) * inv_state * gb[y, 0, 0:1, mine]).astype(BF)
    inv_neigh = as_col(lax.rsqrt((ns[0] + ns[1] + ns[2] + ns[3]) / FEATURES + EPSILON))
    qe[...] = (neigh[:, mine].astype(F32) * inv_neigh * gb[y, 1, 1:2, mine]).astype(BF)

    def project_states(i):
        shared(1, i)
        z = mod4(zh + ORDER[1][i])

        def step(k, carry):
            part = nn(xn[k, :, pl.ds(pl.multiple_of(z * 256, 256), 256)], w[1, k, z].reshape(256, COLS))
            acc1[...] += part
            return carry

        lax.fori_loop(0, 4, step, 0)

    acc1[...] = jnp.zeros_like(acc1)
    slots[1].rest()
    slots[2].forward()
    slots[3].start()
    pl.when(g == 0)(lambda: zout(0))
    slots[2].rest()
    slots[2].pass_far(slots[4])
    slots[3].forward()
    slots[4].start()
    slots[3].rest()
    slots[3].pass_far(slots[4])
    slots[4].forward()
    slots[5].start()
    project_states(0)
    project_states(1)
    project_states(2)
    slots[4].rest()
    project_states(3)
    skv[...] = acc1[...].astype(BF)

    base_span = d * 2

    def spans_of(slot):
        spans = [span[i] - base_span for i in range(4)]
        return jnp.where(
            slot == 0, spans[0], jnp.where(slot == 1, spans[1], jnp.where(slot == 2, spans[2], spans[3]))
        )

    def iota(shape, axis):
        return lax.broadcasted_iota(jnp.int32, shape, axis)

    enc_mask = spans_of(iota((ROWS, TOK), 0) >> 6) == (iota((ROWS, TOK), 1) >> 6)
    slots_t = iota((TOK, ROWS), 1) >> 6
    dec_mask = (spans_of(slots_t) == (iota((TOK, ROWS), 0) >> 6)) & (slots_t < counts[0])

    def softmax(scores, mask):
        scores = jnp.where(mask, scores * SCALE, NEG_LARGE)
        top = jnp.max(scores, axis=-1, keepdims=True)
        raised = jnp.exp(scores - top)
        return raised * (1.0 / jnp.sum(raised, axis=-1, keepdims=True))

    def head(i, second=False):
        start = i * HD + (HALF if second else 0)
        return slice(start, start + HD)

    def mine_head(i):
        return pl.ds(pl.multiple_of(g * HALF + i * HD, HD), HD)

    me8 = y * 2 + g
    for i in range(HEADS):
        probs = softmax(nt(qe[:, head(i)], skv[:, head(i)]), enc_mask)
        pe[i] = probs
        o = nn(probs.astype(BF), skv[:, head(i, True)])
        eb[me8, :, head(i)] = (neigh[:, mine_head(i)].astype(F32) + o).astype(BF)

    def ehalf(grp, rows):
        return lambda r, k: eb.at[mod4(y + r) * 2 + grp, pl.ds(k * rows, rows), :]

    def epart(r, grp, low):
        rows = pl.ds(UP, ROWS - UP) if low else pl.ds(0, UP)
        return eb.at[mod4(y + r) * 2 + grp, rows, :]

    e_slot = comm.alloc(5)

    def relay(i, r):
        comm.send(e_slot + i, epart(r, g, True), epart(r, g, True), partner)

    comm.send(e_slot, epart(0, g, False), epart(0, g, False), partner)
    ring_own, ring_other = Ring(comm, ehalf(g, 128), yp, ym), Ring(comm, ehalf(1 - g, UP // 2), yp, ym)
    ring_own.start()
    relay(4, 0)
    slots[5].forward()
    slots[6].start()
    ring_own.forward()
    comm.recv(e_slot, epart(0, 1 - g, False), partner)
    ring_other.start()
    slots[5].rest()
    slots[5].pass_far(slots[7])
    ring_own.near()
    relay(1, 1)
    relay(2, -1)
    slots[6].forward()
    slots[7].start()
    ring_other.forward()
    ring_own.far()
    relay(3, 2)

    def scaled(h):
        def step(i, carry):
            v = eb[i * 2 + h].astype(F32)
            cols = pl.ds(pl.multiple_of(h * HALF, HALF), HALF)
            en[i * 2 + h] = (v * gb[i, 0, 1:2, cols]).astype(BF)
            return carry + jnp.sum(v * v, axis=1, keepdims=True)

        return lax.fori_loop(0, 4, step, jnp.zeros((ROWS, 1), F32))

    enc_sum = scaled(g)
    slots[6].rest()
    slots[6].pass_far(slots[7])
    ring_other.near()
    ring_other.far()
    slots[7].forward()
    for i, r in ((4, 0), (1, 1), (2, -1), (3, 2)):
        comm.recv(e_slot + i, epart(r, 1 - g, True), partner)
    inv_enc = lax.rsqrt((enc_sum + scaled(1 - g)) / FEATURES + EPSILON)

    acc2[...] = jnp.zeros_like(acc2)

    def project_enc(i):
        shared(0, i)
        z = mod4(zh + ORDER[0][i])

        def step(k, carry):
            cols = pl.ds(pl.multiple_of((z % 2) * 256, 256), 256)
            acc2[...] += nn(en[k * 2 + z // 2, :, cols], w[0, k, z].reshape(256, COLS))
            return carry

        lax.fori_loop(0, 4, step, 0)

    for i in range(3):
        project_enc(i)
    slots[7].rest()
    project_enc(3)
    nkv[...] = (acc2[...] * inv_enc).astype(BF)

    mx_slot = comm.alloc(1)
    rowdot = jnp.zeros((ROWS, 1), F32)
    heads = range(HEADS)
    q = [dq[:, head(i)] for i in heads]
    k = [nkv[:, head(i)] for i in heads]
    v = [nkv[:, head(i, True)] for i in heads]
    ct = [cot[:, mine_head(i)] for i in heads]
    scores = [nt(q[i], k[i]) for i in heads]
    grad_probs = [nt(ct[i], v[i]) for i in heads]
    probs = [softmax(scores[i], dec_mask) for i in heads]
    rounded = [probs[i].astype(BF) for i in heads]
    grad_scores = [
        (probs[i] * (grad_probs[i] - jnp.sum(grad_probs[i] * probs[i], axis=-1, keepdims=True))).astype(BF)
        for i in heads
    ]
    grad_values = [tn(rounded[i], ct[i]) for i in heads]
    grad_keys = [tn(grad_scores[i], q[i]) * SCALE for i in heads]
    for i in heads:
        g2[:, head(i)] = grad_keys[i].astype(BF)
        g2[:, head(i, True)] = grad_values[i].astype(BF)
    def back_enc(r, h):
        b = mod4(y + r) * 2 + h
        pb[b] = nt(g2[...], w[0, b // 2, pl.ds((b % 2) * 2, 2)].reshape(HALF, COLS)).astype(BF)

    def rows_of(low):
        return pl.ds(ROWS - LOW, LOW) if low else pl.ds(0, ROWS - LOW)

    def part_of(r, h, low):
        return pb.at[mod4(y + r) * 2 + h, rows_of(low), :]

    def scatter_of(h, low, j):
        n = LOW if low else ROWS - LOW
        short, whole_rows = pl.ds(0, n // 2), pl.ds(0, n)
        bufs = [rba.at[j, k, short, :] for k in (0, 1)] + [rbb.at[j, k, whole_rows, :] for k in (0, 1)]
        return Scatter(comm, lambda r: part_of(r, h, low), bufs, yp, ym, n)

    away, home, low = scatter_of(1 - g, False, 0), scatter_of(g, False, 1), scatter_of(g, True, 2)
    low_slot = comm.alloc(4)

    def lower(i, r):
        comm.send(low_slot + i, part_of(r, 1 - g, True), lz.at[i], partner)

    def lower_add(i, r):
        comm.recv(low_slot + i, lz.at[i], partner)
        a = part_of(r, g, True)
        a[...] = (a[...].astype(F32) + lz[i].astype(F32)).astype(BF)

    back_enc(2, 1 - g)
    away.first()
    lower(0, 2)
    back_enc(1, 1 - g)
    lower(1, 1)
    back_enc(-1, 1 - g)
    lower(2, -1)
    away.second()
    for i in heads:
        mxs[:, head(i)] = nn(rounded[i], v[i]).astype(BF)
        rowdot = rowdot + jnp.sum(
            grad_keys[i] * k[i].astype(F32) + grad_values[i] * v[i].astype(F32), axis=1, keepdims=True
        )
    mx_copy = comm.copy(mx_slot, mxs, mxr, partner)

    rd[y] = as_row(rowdot)
    rd_base = comm.alloc(4)
    small_start(rd, rd_base)

    back_enc(2, g)
    home.first()
    back_enc(0, 1 - g)
    lower(3, 0)
    back_enc(1, g)
    back_enc(-1, g)
    away.third()
    home.second()
    small_wait(rd, rd_base)
    rdp[0] = rd[0] + rd[1] + rd[2] + rd[3]
    comm.send(rd_base + 3, rdp.at[0], rdp.at[1], partner)
    back_enc(0, g)
    lower_add(0, 2)
    low.first()
    home.third()
    ysum[...] = away.total().astype(BF)
    r3_slot = comm.alloc(1)
    comm.send(r3_slot, ysum, r3, partner)
    lower_add(1, 1)
    lower_add(2, -1)
    low.second()
    low.third()

    @pl.when(g == 1)
    def _():
        mx_copy.start()

    comm.recv(rd_base + 3, rdp.at[1], partner)
    dot_all = as_col(rdp[0] + rdp[1])
    lower_add(3, 0)
    upper_in = home.total()
    comm.recv(r3_slot, r3, partner)
    grad_in = jnp.concatenate([upper_in + r3[...].astype(F32), low.total()], axis=0)
    grad_enc = (
        inv_enc * gb[y, 0, 1:2, mine] * grad_in
        - eb[me8].astype(F32) * (inv_enc * inv_enc * dot_all / FEATURES)
    ).astype(BF)

    rowdot1 = jnp.zeros((TOK, 1), F32)
    q = [qe[:, head(i)] for i in heads]
    k = [skv[:, head(i)] for i in heads]
    v = [skv[:, head(i, True)] for i in heads]
    go = [grad_enc[:, head(i)] for i in heads]
    probs = [pe[i] for i in heads]
    grad_probs = [nt(go[i], v[i]) for i in heads]
    grad_values = [tn(probs[i].astype(BF), go[i]) for i in heads]
    grad_scores = [
        (probs[i] * (grad_probs[i] - jnp.sum(grad_probs[i] * probs[i], axis=-1, keepdims=True))).astype(BF)
        for i in heads
    ]
    grad_keys = [tn(grad_scores[i], q[i]) * SCALE for i in heads]
    for i in heads:
        g1[:, head(i)] = grad_keys[i].astype(BF)
        g1[:, head(i, True)] = grad_values[i].astype(BF)
    def back_state(r, h):
        b = mod4(y + r) * 2 + h
        pb1[b] = nt(g1[...], w[1, b // 2, pl.ds((b % 2) * 2, 2)].reshape(HALF, COLS)).astype(BF)

    def token_part(r, h, low):
        rows = pl.ds(TOK - LOW1, LOW1) if low else pl.ds(0, TOK - LOW1)
        return pb1.at[mod4(y + r) * 2 + h, rows, :]

    def scatter_state(h, low):
        n, j = (LOW1 if low else TOK - LOW1), h * 2 + low
        short, whole_rows = pl.ds(0, n // 2), pl.ds(0, n)
        bufs = [rca.at[j, k, short, :] for k in (0, 1)] + [rcb.at[j, k, whole_rows, :] for k in (0, 1)]
        return Scatter(comm, lambda r: token_part(r, h, low), bufs, yp, ym, n)

    ups = [scatter_state(h, False) for h in range(2)]
    lows = [scatter_state(h, True) for h in range(2)]
    raw_slot = comm.alloc(8)
    raw = {}

    def raw_send(r, h):
        i = h * 4 + r % 4
        raw[r, h] = comm.copy(raw_slot + i, token_part(r, h, True), lz1.at[i], partner)
        pl.when(g == 0)(lambda: raw[r, h].start())

    def raw_add(*pairs):
        @pl.when(g == 1)
        def _():
            for r, h in pairs:
                raw[r, h].wait_recv()
                a = token_part(r, h, True)
                a[...] = (a[...].astype(F32) + lz1[h * 4 + r % 4].astype(F32)).astype(BF)

    for h in range(2):
        back_state(2, h)
        ups[h].first()
        raw_send(2, h)
        back_state(1, h)
        back_state(-1, h)
        ups[h].second()
        raw_send(1, h)
        raw_send(-1, h)
    for h in range(2):
        back_state(0, h)
        raw_send(0, h)
    for i in heads:
        rowdot1 = rowdot1 + jnp.sum(
            grad_keys[i] * k[i].astype(F32) + grad_values[i] * v[i].astype(F32), axis=1, keepdims=True
        )
    rd1[y] = as_row(rowdot1)
    rd1_base = comm.alloc(4)
    small_start(rd1, rd1_base)

    ups[0].third()
    raw_add((2, 0), (2, 1))
    lows[0].first()
    lows[1].first()
    ups[1].third()
    small_wait(rd1, rd1_base)
    rdp1[0] = rd1[0] + rd1[1] + rd1[2] + rd1[3]
    comm.send(rd1_base + 3, rdp1.at[0], rdp1.at[1], partner)
    raw_add((1, 0), (-1, 0), (1, 1), (-1, 1))
    for h in range(2):
        lows[h].second()
    t3_slot = comm.alloc(2)
    t3_copies = [comm.copy(t3_slot + h, ysum1.at[h], t3.at[h], partner) for h in range(2)]
    for h in range(2):
        ysum1[h] = ups[h].total().astype(BF)

        @pl.when(g == 0)
        def _(h=h):
            t3_copies[h].start()
            for r in (1, -1):
                raw[r, h].wait_send()

        lows[h].third()

    raw_add((0, 0), (0, 1))
    low_sums = [lows[h].total() for h in range(2)]
    comm.recv(rd1_base + 3, rdp1.at[1], partner)

    @pl.when(g == 0)
    def _():
        mx_copy.wait_recv()
        for h in range(2):
            heads_out = mxr if h == 1 else mxs
            cols = slice(h * HALF, (h + 1) * HALF)
            out[:, cols] = states[:, cols].astype(F32) + heads_out[...].astype(F32)
        for copy in (*t3_copies, *(raw[r, h] for h in range(2) for r in (2, 0))):
            copy.wait_send()

    @pl.when(g == 1)
    def _():
        dot_state = as_col(rdp1[0] + rdp1[1])
        factor = inv_state * inv_state * dot_state / FEATURES
        for h in range(2):
            t3_copies[h].wait_recv()
            cols = slice(h * HALF, (h + 1) * HALF)
            upper = ysum1[h].astype(F32) + t3[h].astype(F32)
            total = jnp.concatenate([upper, low_sums[h]], axis=0)
            out[:, cols] = (
                inv_state * gb[y, 1, 0:1, cols] * total - states[:, cols].astype(F32) * factor
            )
        mx_copy.wait_send()

    comm.drain()
    either(lambda grp: ([make().wait_send() for make in zsent[grp]], None)[1])


def per_device(states, neighbours, cotangent, span_of, counts, kv_weight, gains):
    wide = kv_weight.reshape(TOK, 2 * COLS)
    vmem, smem, hbm = (
        pl.BlockSpec(memory_space=m) for m in (pltpu.VMEM, pltpu.SMEM, pl.ANY)
    )

    def bf(*shape):
        return pltpu.VMEM(shape, BF)

    def f32(*shape):
        return pltpu.VMEM(shape, F32)

    scratch = [
        bf(2, 4, 4, 2, TOK, COLS),
        bf(TOK, COLS),
        bf(TOK, COLS),
        bf(ROWS, COLS),
        bf(TOK, COLS),
        bf(4, TOK, COLS),
        bf(4, TOK, COLS),
        f32(4, 2, 8, COLS),
        f32(4, 8, ROWS),
        bf(8, ROWS, HALF),
        bf(8, ROWS, HALF),
        f32(TOK, COLS),
        bf(TOK, COLS),
        bf(ROWS, HALF),
        f32(HEADS, ROWS, TOK),
        f32(ROWS, COLS),
        bf(ROWS, COLS),
        bf(TOK, HALF),
        bf(ROWS, COLS),
        bf(8, ROWS, HALF),
        bf(4, LOW, HALF),
        bf(3, 2, (ROWS - LOW) // 2, HALF),
        bf(3, 2, ROWS - LOW, HALF),
        bf(ROWS - LOW, HALF),
        bf(ROWS - LOW, HALF),
        bf(TOK, COLS),
        bf(8, TOK, HALF),
        bf(8, LOW1, HALF),
        bf(4, 2, (TOK - LOW1) // 2, HALF),
        bf(4, 2, TOK - LOW1, HALF),
        bf(2, TOK - LOW1, HALF),
        bf(2, TOK - LOW1, HALF),
        f32(4, 8, ROWS),
        f32(2, 8, ROWS),
        f32(4, 8, TOK),
        f32(2, 8, TOK),
        bf(TOK, HALF),
        bf(TOK, HALF),
        pltpu.SemaphoreType.DMA((SEMS,)),
        pltpu.SemaphoreType.DMA((SEMS,)),
        pltpu.SemaphoreType.DMA((7,)),
    ]
    result = pl.pallas_call(
        kernel,
        out_shape=jax.ShapeDtypeStruct((TOK, COLS), F32),
        in_specs=[hbm, hbm, hbm, hbm, smem, smem, vmem],
        out_specs=vmem,
        scratch_shapes=scratch,
        compiler_params=pltpu.CompilerParams(
            collective_id=0, has_side_effects=True, vmem_limit_bytes=60 * 1024 * 1024
        ),
        name="spanned_attention",
    )(
        wide,
        states,
        neighbours.reshape(ROWS, COLS),
        cotangent,
        span_of,
        counts,
        gains.reshape(2, COLS),
    )
    return result[None]


def solution(mesh):
    return jax.shard_map(
        per_device,
        mesh=mesh,
        in_specs=(
            P("dp", "mp"),
            P("dp", None, "mp"),
            P("dp", "mp"),
            P("dp"),
            P("dp"),
            P("group", "dp", None, "mp"),
            P("group", None, "mp"),
        ),
        out_specs=P("group", "dp", "mp"),
        check_vma=False,
    )
```

```python
import functools

import jax
import jax.numpy as jnp
from jax import lax
from jax.experimental import pallas as pl
from jax.experimental.pallas import tpu as pltpu
from jax.sharding import PartitionSpec as P

HD = 128
FEATURES = 4096
CH = 64
EPSILON = 1e-05
NEG_LARGE = -1e30
TOK = 128
ROWS = 256
COLS = 1024
HALF = 512
HEADS = 4
SCALE = HD ** (-0.5)
BF = jnp.bfloat16
F32 = jnp.float32
SEMS = 320
AROWS = TOK
FAR_BY_Z = (4,)
UP = 160
LOW = 128
LOW1 = 32
SPLIT = 64


def nt(a, b):
    return lax.dot_general(a, b, (((1,), (1,)), ((), ())), preferred_element_type=F32)


def nn(a, b):
    return lax.dot_general(a, b, (((1,), (0,)), ((), ())), preferred_element_type=F32)


def tn(a, b):
    return lax.dot_general(a, b, (((0,), (0,)), ((), ())), preferred_element_type=F32)


class Comm:
    def __init__(self, ssem, rsem):
        self.ssem, self.rsem = ssem, rsem
        self.used, self.sent = 0, []

    def alloc(self, count):
        base = self.used
        self.used += count
        assert self.used <= SEMS
        return base

    def copy(self, slot, src, dst, dev):
        return pltpu.make_async_remote_copy(
            src_ref=src,
            dst_ref=dst,
            send_sem=self.ssem.at[slot],
            recv_sem=self.rsem.at[slot],
            device_id=dev,
            device_id_type=pl.DeviceIdType.MESH,
        )

    def send(self, slot, src, dst, dev):
        copy = self.copy(slot, src, dst, dev)
        copy.start()
        self.sent.append(copy)

    def recv(self, slot, dst, dev):
        self.copy(slot, dst, dst, dev).wait_recv()

    def drain(self):
        for copy in self.sent:
            copy.wait_send()


class Ring:
    def __init__(self, comm, half, plus, minus):
        self.comm, self.half, self.plus, self.minus = comm, half, plus, minus
        self.base = comm.alloc(6)

    def start(self):
        for slot, k, dev in ((0, 0, self.plus), (2, 1, self.minus), (1, 1, self.plus), (3, 0, self.minus)):
            self.comm.send(self.base + slot, self.half(0, k), self.half(0, k), dev)

    def forward(self):
        self.comm.recv(self.base, self.half(-1, 0), self.minus)
        self.comm.send(self.base + 4, self.half(-1, 0), self.half(-1, 0), self.plus)
        self.comm.recv(self.base + 2, self.half(1, 1), self.plus)
        self.comm.send(self.base + 5, self.half(1, 1), self.half(1, 1), self.minus)

    def near(self):
        self.comm.recv(self.base + 1, self.half(-1, 1), self.minus)
        self.comm.recv(self.base + 3, self.half(1, 0), self.plus)

    def far(self):
        self.comm.recv(self.base + 4, self.half(2, 0), self.minus)
        self.comm.recv(self.base + 5, self.half(2, 1), self.plus)


class Scatter:
    def __init__(self, comm, part, bufs, plus, minus, rows):
        self.comm, self.part, self.plus, self.minus, self.n = comm, part, plus, minus, rows // 2
        self.from_minus, self.from_plus, self.last_minus, self.last_plus = bufs
        self.base = comm.alloc(6)

    def lo(self, ref):
        return ref.at[pl.ds(0, self.n), :]

    def hi(self, ref):
        return ref.at[pl.ds(self.n, self.n), :]

    def first(self):
        self.comm.send(self.base, self.lo(self.part(2)), self.from_minus, self.plus)
        self.comm.send(self.base + 1, self.hi(self.part(2)), self.from_plus, self.minus)

    def second(self):
        self.comm.send(self.base + 2, self.hi(self.part(1)), self.hi(self.last_minus), self.plus)
        self.comm.send(self.base + 3, self.lo(self.part(-1)), self.lo(self.last_plus), self.minus)

    def third(self):
        self.comm.recv(self.base, self.from_minus, self.minus)
        a = self.lo(self.part(1))
        a[...] = (a[...].astype(F32) + self.from_minus[...].astype(F32)).astype(BF)
        self.comm.send(self.base + 4, a, self.lo(self.last_minus), self.plus)
        self.comm.recv(self.base + 1, self.from_plus, self.plus)
        b = self.hi(self.part(-1))
        b[...] = (b[...].astype(F32) + self.from_plus[...].astype(F32)).astype(BF)
        self.comm.send(self.base + 5, b, self.hi(self.last_plus), self.minus)

    def total(self):
        self.comm.recv(self.base + 2, self.hi(self.last_minus), self.minus)
        self.comm.recv(self.base + 3, self.lo(self.last_plus), self.plus)
        self.comm.recv(self.base + 4, self.lo(self.last_minus), self.minus)
        self.comm.recv(self.base + 5, self.hi(self.last_plus), self.plus)
        return (
            self.part(0)[...].astype(F32)
            + self.last_minus[...].astype(F32)
            + self.last_plus[...].astype(F32)
        )


def as_row(col):
    return jnp.transpose(jnp.broadcast_to(col, (col.shape[0], 128)))[0:8, :]


def as_col(row):
    return jnp.transpose(jnp.broadcast_to(row[0:1, :], (128, row.shape[1])))[:, 0:1]


def kernel(
    wide, states_in, neigh_in, cot_in, span, counts, gains, out,
    w, theirs, states, neigh, cot, sx, xn, gb, ns, eb, en, acc1, skv, qe, pe, acc2, nkv, dq, g2, pb, lz, rba, rbb, r3, ysum,
    g1, pb1, lz1, rca, rcb, t3, ysum1, rd, rdp, rd1, rdp1, mxs, mxr,
    ssem, rsem, lsem,
):
    g = lax.axis_index("group")
    d = lax.axis_index("dp")
    y = lax.axis_index("mp")
    x, zh, c = d // 8, (d // 2) % 4, d % 2
    comm = Comm(ssem, rsem)

    def mod4(v):
        return (v + 4) % 4

    def at_x(r):
        return {"dp": mod4(x + r) * 8 + zh * 2 + c}

    def at_z(r):
        return {"dp": x * 8 + mod4(zh + r) * 2 + c}

    def at_y(r):
        return {"mp": mod4(y + r)}

    partner = {"group": 1 - g}
    sibling = {"dp": d + 1 - 2 * c}
    xp, xm, zp, zm, yp, ym, y2 = at_x(1), at_x(-1), at_z(1), at_z(-1), at_y(1), at_y(-1), at_y(2)

    across = {"group": 1 - g, "dp": x * 8 + mod4(zh + 2 * g - 1) * 2 + c}
    fetch = [
        pltpu.make_async_copy(src, dst, lsem.at[i])
        for i, (src, dst) in enumerate(((states_in, states), (neigh_in, neigh), (cot_in, cot)))
    ]
    local = []
    for i, (grp, dst) in enumerate(((g, w.at[g, x, zh, c]), (1 - g, theirs))):
        for pair in range(2):
            cols = pl.ds(pl.multiple_of(pair * COLS + grp * HALF, HALF), HALF)
            to = dst.at[:, pl.ds(pair * HALF, HALF)]
            local.append(pltpu.make_async_copy(wide.at[:, cols], to, lsem.at[3 + 2 * i + pair]))
            local[-1].start()
    for copy in fetch:
        copy.start()
    barrier = pltpu.get_barrier_semaphore()
    peers = (partner, sibling, xp, xm, zp, zm, yp, ym, y2, across)
    for dev in peers:
        pl.semaphore_signal(barrier, inc=1, device_id=dev, device_id_type=pl.DeviceIdType.MESH)
    for copy in fetch:
        copy.wait()
    nf = neigh[...].astype(F32)
    sq_rows = as_row(jnp.sum(nf * nf, axis=1, keepdims=True))
    sx[y] = states[...]
    even = lax.broadcasted_iota(jnp.int32, (8, COLS), 0) % 2 == 0
    gb[y, g] = jnp.where(even, gains[0:1, :], gains[1:2, :])
    for copy in local:
        copy.wait()
    pl.semaphore_wait(barrier, len(peers))

    ORDER = {1: (0, -1, 1, 2), 0: (0, 1, -1, 2)}
    PLAN = {
        1: [(1, 0), (0, 0), (1, 1), (1, 2), (1, 3), (0, 1), (0, 2), (0, 3)],
        0: [(0, 0), (1, 0), (1, 1), (1, 2), (1, 3), (0, 1), (0, 2), (0, 3)],
    }
    zbase = {m: comm.alloc(10) for m in (0, 1)}
    zsent = {0: [], 1: []}

    def whole(m, rx, rz, core):
        return w.at[m, mod4(x + rx), mod4(zh + rz), core]

    def main(m, rx, rz, core):
        return whole(m, rx, rz, core).at[pl.ds(0, AROWS), :]

    def main_half(m, rx, rz, k):
        rows = pl.ds(0, SPLIT) if k == 0 else pl.ds(SPLIT, AROWS - SPLIT)
        return whole(m, rx, rz, c).at[rows, :]

    def either(fn):
        for grp in (0, 1):
            pl.when(g == grp)(functools.partial(fn, grp))

    def zhalf(m, rz, k):
        return main_half(m, 0, rz, k)

    def zsend(grp, slot, ref, dev, src=None):
        def make():
            dst = ref()
            return comm.copy(slot, dst if src is None else src(), dst, dev)

        make().start()
        zsent[grp].append(make)

    def zpartner(grp):
        zsend(grp, zbase[grp] + 6, lambda: whole(grp, 0, 0, c), partner, lambda: theirs)

    def zout(grp):
        m, base = grp, zbase[grp]
        zsend(
            grp, base + 7, lambda: main(m, 0, 0, c), across, lambda: theirs.at[pl.ds(0, AROWS), :]
        )
        for slot, k, dev in ((0, 0, zp), (2, 1, zm), (1, 1, zp), (3, 0, zm)):
            zsend(grp, base + slot, lambda k=k: zhalf(m, 0, k), dev)

    def zarrive(grp, m, i):
        base, rz = zbase[m], ORDER[m][i]
        if grp == m:
            if i == 0:
                return
            if i == 1:
                comm.recv(base, zhalf(m, -1, 0), zm)
                zsend(grp, base + 4, lambda: zhalf(m, -1, 0), zp)
                comm.recv(base + 2, zhalf(m, 1, 1), zp)
                zsend(grp, base + 5, lambda: zhalf(m, 1, 1), zm)
            if rz == -1:
                comm.recv(base + 1, zhalf(m, -1, 1), zm)
            elif rz == 1:
                comm.recv(base + 3, zhalf(m, 1, 0), zp)
            else:
                comm.recv(base + 4, zhalf(m, 2, 0), zm)
                comm.recv(base + 5, zhalf(m, 2, 1), zp)
            return
        if i == 0:
            comm.recv(base + 6, whole(m, 0, 0, c), partner)
            if m == 1:
                zsend(grp, base + 8, lambda: main(m, 0, 0, c), zm)
        elif i == 1:
            if m == 0:
                zsend(grp, base + 8, lambda: main(m, 0, 0, c), zp)
            comm.recv(base + 7, main(m, 0, rz, c), across)
            zsend(grp, base + 9, lambda: main(m, 0, rz, c), zp if m == 1 else zm)
        else:
            comm.recv(base + 6 + i, main(m, 0, rz, c), zp)

    def plan(grp, s):
        m, i = PLAN[grp][s]
        return m, ORDER[m][i]

    class Slot:
        def __init__(self, s):
            (m0, r0), (m1, r1) = plan(0, s), plan(1, s)
            self.m_, self.arrival = PLAN[0][s]
            self.s, self.m, self.rz = s, m0 + (m1 - m0) * g, r0 + (r1 - r0) * g
            self.ring = Ring(comm, self.half, xp, xm)
            self.sib = comm.alloc(4)
            self.far = comm.alloc(2)

        def half(self, r, k):
            return main_half(self.m, r, self.rz, k)

        def share(self, *rels):
            for rx in rels:
                block = main(self.m, rx, self.rz, c)
                comm.send(self.sib + rx % 4, block, block, sibling)

        def start(self):
            either(lambda grp: zarrive(grp, *PLAN[grp][self.s]))
            self.ring.start()
            self.share(0)

        def forward(self):
            if self.s not in FAR_BY_Z:
                self.ring.forward()

        def rest(self):
            if self.s in FAR_BY_Z:
                comm.recv(self.ring.base, self.half(-1, 0), xm)
                comm.recv(self.ring.base + 2, self.half(1, 1), xp)
            self.ring.near()
            self.share(-1, 1)
            if self.s in FAR_BY_Z:
                comm.recv(self.far, self.half(2, 0), zm)
                comm.recv(self.far + 1, self.half(2, 1), zp)
            else:
                self.ring.far()
            self.share(2)

        def pass_far(self, to):
            if to.s in FAR_BY_Z:
                k, dev = (0, zp) if ORDER[to.m_][self.arrival] == -1 else (1, zm)
                ref = self.half(2, k)
                comm.send(to.far + k, ref, ref, dev)

    slots = [Slot(s) for s in range(8)]
    sib_first = slots[0].sib
    sib_step = slots[1].sib - slots[0].sib

    def shared(m, i):
        s0, s1 = (PLAN[grp].index((m, i)) for grp in (0, 1))
        for rx in range(4):
            comm.recv(
                sib_first + (s0 + (s1 - s0) * g) * sib_step + rx,
                main(m, rx, ORDER[m][i], 1 - c),
                sibling,
            )

    either(zpartner)
    slots[0].start()

    def shalf(r, k):
        return sx.at[mod4(y + r), pl.ds(k * 64, 64), :]

    sring = Ring(comm, shalf, yp, ym)
    sring.start()
    gain_slot = comm.alloc(4)
    comm.send(gain_slot, gb.at[y, g], gb.at[y, g], partner)

    def small_start(buf, base):
        for i, (r, dev) in enumerate(((1, yp), (-1, ym), (2, y2))):
            comm.send(base + i, buf.at[y], buf.at[y], dev)

    def small_wait(buf, base):
        for i, (r, dev) in enumerate(((-1, ym), (1, yp), (2, y2))):
            comm.recv(base + i, buf.at[mod4(y + r)], dev)

    slots[0].forward()
    pl.when(g == 1)(lambda: zout(1))
    sring.forward()
    ns[y] = sq_rows
    ns_base = comm.alloc(3)
    small_start(ns, ns_base)
    comm.recv(gain_slot, gb.at[y, 1 - g], partner)
    small_start(gb, gain_slot + 1)
    slots[1].start()
    slots[0].rest()
    sring.near()
    sring.far()
    small_wait(ns, ns_base)
    small_wait(gb, gain_slot + 1)
    slots[1].forward()
    slots[2].start()

    mine = pl.ds(pl.multiple_of(g * HALF, HALF), HALF)
    sums = jnp.zeros((TOK, 1), F32)
    for i in range(4):
        v = sx[i].astype(F32)
        sums = sums + jnp.sum(v * v, axis=1, keepdims=True)
    inv_state = lax.rsqrt(sums / FEATURES + EPSILON)

    def norm_states(i, carry):
        xn[i] = (sx[i].astype(F32) * inv_state * gb[i, 1, 0:1, :]).astype(BF)
        return carry

    lax.fori_loop(0, 4, norm_states, 0)
    dq[...] = (states[:, mine].astype(F32) * inv_state * gb[y, 0, 0:1, mine]).astype(BF)
    inv_neigh = as_col(lax.rsqrt((ns[0] + ns[1] + ns[2] + ns[3]) / FEATURES + EPSILON))
    qe[...] = (neigh[:, mine].astype(F32) * inv_neigh * gb[y, 1, 1:2, mine]).astype(BF)

    def project_states(i):
        shared(1, i)
        z = mod4(zh + ORDER[1][i])

        def step(k, carry):
            part = nn(xn[k, :, pl.ds(pl.multiple_of(z * 256, 256), 256)], w[1, k, z].reshape(256, COLS))
            acc1[...] += part
            return carry

        lax.fori_loop(0, 4, step, 0)

    acc1[...] = jnp.zeros_like(acc1)
    slots[1].rest()
    slots[2].forward()
    pl.when(g == 0)(lambda: zout(0))
    slots[3].start()
    slots[2].rest()
    slots[2].pass_far(slots[4])
    slots[3].forward()
    slots[4].start()
    slots[3].rest()
    slots[3].pass_far(slots[4])
    slots[4].forward()
    slots[5].start()
    project_states(0)
    project_states(1)
    project_states(2)
    slots[4].rest()
    project_states(3)
    skv[...] = acc1[...].astype(BF)

    base_span = d * 2

    def spans_of(slot):
        spans = [span[i] - base_span for i in range(4)]
        return jnp.where(
            slot == 0, spans[0], jnp.where(slot == 1, spans[1], jnp.where(slot == 2, spans[2], spans[3]))
        )

    def iota(shape, axis):
        return lax.broadcasted_iota(jnp.int32, shape, axis)

    enc_mask = spans_of(iota((ROWS, TOK), 0) >> 6) == (iota((ROWS, TOK), 1) >> 6)
    slots_t = iota((TOK, ROWS), 1) >> 6
    dec_mask = (spans_of(slots_t) == (iota((TOK, ROWS), 0) >> 6)) & (slots_t < counts[0])

    def softmax(scores, mask):
        scores = jnp.where(mask, scores * SCALE, NEG_LARGE)
        top = jnp.max(scores, axis=-1, keepdims=True)
        raised = jnp.exp(scores - top)
        return raised * (1.0 / jnp.sum(raised, axis=-1, keepdims=True))

    def head(i, second=False):
        start = i * HD + (HALF if second else 0)
        return slice(start, start + HD)

    def mine_head(i):
        return pl.ds(pl.multiple_of(g * HALF + i * HD, HD), HD)

    me8 = y * 2 + g
    for i in range(HEADS):
        probs = softmax(nt(qe[:, head(i)], skv[:, head(i)]), enc_mask)
        pe[i] = probs
        o = nn(probs.astype(BF), skv[:, head(i, True)])
        eb[me8, :, head(i)] = (neigh[:, mine_head(i)].astype(F32) + o).astype(BF)

    def ehalf(grp, rows):
        return lambda r, k: eb.at[mod4(y + r) * 2 + grp, pl.ds(k * rows, rows), :]

    def epart(r, grp, low):
        rows = pl.ds(UP, ROWS - UP) if low else pl.ds(0, UP)
        return eb.at[mod4(y + r) * 2 + grp, rows, :]

    e_slot = comm.alloc(5)

    def relay(i, r):
        comm.send(e_slot + i, epart(r, g, True), epart(r, g, True), partner)

    comm.send(e_slot, epart(0, g, False), epart(0, g, False), partner)
    ring_own, ring_other = Ring(comm, ehalf(g, 128), yp, ym), Ring(comm, ehalf(1 - g, UP // 2), yp, ym)
    ring_own.start()
    relay(4, 0)
    slots[5].forward()
    slots[6].start()
    ring_own.forward()
    comm.recv(e_slot, epart(0, 1 - g, False), partner)
    ring_other.start()
    slots[5].rest()
    slots[5].pass_far(slots[7])
    ring_own.near()
    relay(1, 1)
    relay(2, -1)
    slots[6].forward()
    slots[7].start()
    ring_other.forward()
    ring_own.far()
    relay(3, 2)

    def scaled(h):
        def step(i, carry):
            v = eb[i * 2 + h].astype(F32)
            cols = pl.ds(pl.multiple_of(h * HALF, HALF), HALF)
            en[i * 2 + h] = (v * gb[i, 0, 1:2, cols]).astype(BF)
            return carry + jnp.sum(v * v, axis=1, keepdims=True)

        return lax.fori_loop(0, 4, step, jnp.zeros((ROWS, 1), F32))

    enc_sum = scaled(g)
    slots[6].rest()
    slots[6].pass_far(slots[7])
    ring_other.near()
    ring_other.far()
    slots[7].forward()
    for i, r in ((4, 0), (1, 1), (2, -1), (3, 2)):
        comm.recv(e_slot + i, epart(r, 1 - g, True), partner)
    inv_enc = lax.rsqrt((enc_sum + scaled(1 - g)) / FEATURES + EPSILON)

    acc2[...] = jnp.zeros_like(acc2)

    def project_enc(i):
        shared(0, i)
        z = mod4(zh + ORDER[0][i])

        def step(k, carry):
            cols = pl.ds(pl.multiple_of((z % 2) * 256, 256), 256)
            acc2[...] += nn(en[k * 2 + z // 2, :, cols], w[0, k, z].reshape(256, COLS))
            return carry

        lax.fori_loop(0, 4, step, 0)

    for i in range(3):
        project_enc(i)
    slots[7].rest()
    project_enc(3)
    nkv[...] = (acc2[...] * inv_enc).astype(BF)

    mx_slot = comm.alloc(1)
    rowdot = jnp.zeros((ROWS, 1), F32)
    heads = range(HEADS)
    q = [dq[:, head(i)] for i in heads]
    k = [nkv[:, head(i)] for i in heads]
    v = [nkv[:, head(i, True)] for i in heads]
    ct = [cot[:, mine_head(i)] for i in heads]
    scores = [nt(q[i], k[i]) for i in heads]
    grad_probs = [nt(ct[i], v[i]) for i in heads]
    probs = [softmax(scores[i], dec_mask) for i in heads]
    rounded = [probs[i].astype(BF) for i in heads]
    grad_scores = [
        (probs[i] * (grad_probs[i] - jnp.sum(grad_probs[i] * probs[i], axis=-1, keepdims=True))).astype(BF)
        for i in heads
    ]
    grad_values = [tn(rounded[i], ct[i]) for i in heads]
    grad_keys = [tn(grad_scores[i], q[i]) * SCALE for i in heads]
    for i in heads:
        g2[:, head(i)] = grad_keys[i].astype(BF)
        g2[:, head(i, True)] = grad_values[i].astype(BF)
    def back_enc(r, h):
        b = mod4(y + r) * 2 + h
        pb[b] = nt(g2[...], w[0, b // 2, pl.ds((b % 2) * 2, 2)].reshape(HALF, COLS)).astype(BF)

    def rows_of(low):
        return pl.ds(ROWS - LOW, LOW) if low else pl.ds(0, ROWS - LOW)

    def part_of(r, h, low):
        return pb.at[mod4(y + r) * 2 + h, rows_of(low), :]

    def scatter_of(h, low, j):
        n = LOW if low else ROWS - LOW
        short, whole_rows = pl.ds(0, n // 2), pl.ds(0, n)
        bufs = [rba.at[j, k, short, :] for k in (0, 1)] + [rbb.at[j, k, whole_rows, :] for k in (0, 1)]
        return Scatter(comm, lambda r: part_of(r, h, low), bufs, yp, ym, n)

    away, home, low = scatter_of(1 - g, False, 0), scatter_of(g, False, 1), scatter_of(g, True, 2)
    low_slot = comm.alloc(4)

    def lower(i, r):
        comm.send(low_slot + i, part_of(r, 1 - g, True), lz.at[i], partner)

    def lower_add(i, r):
        comm.recv(low_slot + i, lz.at[i], partner)
        a = part_of(r, g, True)
        a[...] = (a[...].astype(F32) + lz[i].astype(F32)).astype(BF)

    back_enc(2, 1 - g)
    away.first()
    lower(0, 2)
    back_enc(1, 1 - g)
    lower(1, 1)
    back_enc(-1, 1 - g)
    lower(2, -1)
    away.second()
    for i in heads:
        mxs[:, head(i)] = nn(rounded[i], v[i]).astype(BF)
        rowdot = rowdot + jnp.sum(
            grad_keys[i] * k[i].astype(F32) + grad_values[i] * v[i].astype(F32), axis=1, keepdims=True
        )
    mx_copy = comm.copy(mx_slot, mxs, mxr, partner)

    rd[y] = as_row(rowdot)
    rd_base = comm.alloc(4)
    small_start(rd, rd_base)

    back_enc(2, g)
    home.first()
    back_enc(0, 1 - g)
    lower(3, 0)
    back_enc(1, g)
    back_enc(-1, g)
    away.third()
    home.second()
    small_wait(rd, rd_base)
    rdp[0] = rd[0] + rd[1] + rd[2] + rd[3]
    comm.send(rd_base + 3, rdp.at[0], rdp.at[1], partner)
    back_enc(0, g)
    lower_add(0, 2)
    low.first()
    home.third()
    ysum[...] = away.total().astype(BF)
    r3_slot = comm.alloc(1)
    comm.send(r3_slot, ysum, r3, partner)
    lower_add(1, 1)
    lower_add(2, -1)
    low.second()
    low.third()

    @pl.when(g == 1)
    def _():
        mx_copy.start()

    comm.recv(rd_base + 3, rdp.at[1], partner)
    dot_all = as_col(rdp[0] + rdp[1])
    lower_add(3, 0)
    upper_in = home.total()
    comm.recv(r3_slot, r3, partner)
    grad_in = jnp.concatenate([upper_in + r3[...].astype(F32), low.total()], axis=0)
    grad_enc = (
        inv_enc * gb[y, 0, 1:2, mine] * grad_in
        - eb[me8].astype(F32) * (inv_enc * inv_enc * dot_all / FEATURES)
    ).astype(BF)

    rowdot1 = jnp.zeros((TOK, 1), F32)
    q = [qe[:, head(i)] for i in heads]
    k = [skv[:, head(i)] for i in heads]
    v = [skv[:, head(i, True)] for i in heads]
    go = [grad_enc[:, head(i)] for i in heads]
    probs = [pe[i] for i in heads]
    grad_probs = [nt(go[i], v[i]) for i in heads]
    grad_values = [tn(probs[i].astype(BF), go[i]) for i in heads]
    grad_scores = [
        (probs[i] * (grad_probs[i] - jnp.sum(grad_probs[i] * probs[i], axis=-1, keepdims=True))).astype(BF)
        for i in heads
    ]
    grad_keys = [tn(grad_scores[i], q[i]) * SCALE for i in heads]
    for i in heads:
        g1[:, head(i)] = grad_keys[i].astype(BF)
        g1[:, head(i, True)] = grad_values[i].astype(BF)
    def back_state(r, h):
        b = mod4(y + r) * 2 + h
        pb1[b] = nt(g1[...], w[1, b // 2, pl.ds((b % 2) * 2, 2)].reshape(HALF, COLS)).astype(BF)

    def token_part(r, h, low):
        rows = pl.ds(TOK - LOW1, LOW1) if low else pl.ds(0, TOK - LOW1)
        return pb1.at[mod4(y + r) * 2 + h, rows, :]

    def scatter_state(h, low):
        n, j = (LOW1 if low else TOK - LOW1), h * 2 + low
        short, whole_rows = pl.ds(0, n // 2), pl.ds(0, n)
        bufs = [rca.at[j, k, short, :] for k in (0, 1)] + [rcb.at[j, k, whole_rows, :] for k in (0, 1)]
        return Scatter(comm, lambda r: token_part(r, h, low), bufs, yp, ym, n)

    ups = [scatter_state(h, False) for h in range(2)]
    lows = [scatter_state(h, True) for h in range(2)]
    raw_slot = comm.alloc(8)
    raw = {}

    def raw_send(r, h):
        i = h * 4 + r % 4
        raw[r, h] = comm.copy(raw_slot + i, token_part(r, h, True), lz1.at[i], partner)
        pl.when(g == 0)(lambda: raw[r, h].start())

    def raw_add(*pairs):
        @pl.when(g == 1)
        def _():
            for r, h in pairs:
                raw[r, h].wait_recv()
                a = token_part(r, h, True)
                a[...] = (a[...].astype(F32) + lz1[h * 4 + r % 4].astype(F32)).astype(BF)

    for h in range(2):
        back_state(2, h)
        ups[h].first()
        raw_send(2, h)
        back_state(1, h)
        back_state(-1, h)
        ups[h].second()
        raw_send(1, h)
        raw_send(-1, h)
    for h in range(2):
        back_state(0, h)
        raw_send(0, h)
    for i in heads:
        rowdot1 = rowdot1 + jnp.sum(
            grad_keys[i] * k[i].astype(F32) + grad_values[i] * v[i].astype(F32), axis=1, keepdims=True
        )
    rd1[y] = as_row(rowdot1)
    rd1_base = comm.alloc(4)
    small_start(rd1, rd1_base)

    ups[0].third()
    raw_add((2, 0), (2, 1))
    lows[0].first()
    lows[1].first()
    ups[1].third()
    small_wait(rd1, rd1_base)
    rdp1[0] = rd1[0] + rd1[1] + rd1[2] + rd1[3]
    comm.send(rd1_base + 3, rdp1.at[0], rdp1.at[1], partner)
    raw_add((1, 0), (-1, 0), (1, 1), (-1, 1))
    for h in range(2):
        lows[h].second()
    t3_slot = comm.alloc(2)
    t3_copies = [comm.copy(t3_slot + h, ysum1.at[h], t3.at[h], partner) for h in range(2)]
    for h in range(2):
        ysum1[h] = ups[h].total().astype(BF)

        @pl.when(g == 0)
        def _(h=h):
            t3_copies[h].start()
            for r in (1, -1):
                raw[r, h].wait_send()

        lows[h].third()

    raw_add((0, 0), (0, 1))
    low_sums = [lows[h].total() for h in range(2)]
    comm.recv(rd1_base + 3, rdp1.at[1], partner)

    @pl.when(g == 0)
    def _():
        mx_copy.wait_recv()
        for h in range(2):
            heads_out = mxr if h == 1 else mxs
            cols = slice(h * HALF, (h + 1) * HALF)
            out[:, cols] = (states[:, cols].astype(F32) + heads_out[...].astype(F32)).astype(BF)
        for copy in (*t3_copies, *(raw[r, h] for h in range(2) for r in (2, 0))):
            copy.wait_send()

    @pl.when(g == 1)
    def _():
        dot_state = as_col(rdp1[0] + rdp1[1])
        factor = inv_state * inv_state * dot_state / FEATURES
        for h in range(2):
            t3_copies[h].wait_recv()
            cols = slice(h * HALF, (h + 1) * HALF)
            upper = ysum1[h].astype(F32) + t3[h].astype(F32)
            total = jnp.concatenate([upper, low_sums[h]], axis=0)
            out[:, cols] = (
                inv_state * gb[y, 1, 0:1, cols] * total - states[:, cols].astype(F32) * factor
            ).astype(BF)
        mx_copy.wait_send()

    comm.drain()
    either(lambda grp: ([make().wait_send() for make in zsent[grp]], None)[1])


def per_device(states, neighbours, cotangent, span_of, counts, kv_weight, gains):
    wide = kv_weight.reshape(TOK, 2 * COLS)
    vmem, smem, hbm = (
        pl.BlockSpec(memory_space=m) for m in (pltpu.VMEM, pltpu.SMEM, pl.ANY)
    )

    def bf(*shape):
        return pltpu.VMEM(shape, BF)

    def f32(*shape):
        return pltpu.VMEM(shape, F32)

    scratch = [
        bf(2, 4, 4, 2, TOK, COLS),
        bf(TOK, COLS),
        bf(TOK, COLS),
        bf(ROWS, COLS),
        bf(TOK, COLS),
        bf(4, TOK, COLS),
        bf(4, TOK, COLS),
        f32(4, 2, 8, COLS),
        f32(4, 8, ROWS),
        bf(8, ROWS, HALF),
        bf(8, ROWS, HALF),
        f32(TOK, COLS),
        bf(TOK, COLS),
        bf(ROWS, HALF),
        f32(HEADS, ROWS, TOK),
        f32(ROWS, COLS),
        bf(ROWS, COLS),
        bf(TOK, HALF),
        bf(ROWS, COLS),
        bf(8, ROWS, HALF),
        bf(4, LOW, HALF),
        bf(3, 2, (ROWS - LOW) // 2, HALF),
        bf(3, 2, ROWS - LOW, HALF),
        bf(ROWS - LOW, HALF),
        bf(ROWS - LOW, HALF),
        bf(TOK, COLS),
        bf(8, TOK, HALF),
        bf(8, LOW1, HALF),
        bf(4, 2, (TOK - LOW1) // 2, HALF),
        bf(4, 2, TOK - LOW1, HALF),
        bf(2, TOK - LOW1, HALF),
        bf(2, TOK - LOW1, HALF),
        f32(4, 8, ROWS),
        f32(2, 8, ROWS),
        f32(4, 8, TOK),
        f32(2, 8, TOK),
        bf(TOK, HALF),
        bf(TOK, HALF),
        pltpu.SemaphoreType.DMA((SEMS,)),
        pltpu.SemaphoreType.DMA((SEMS,)),
        pltpu.SemaphoreType.DMA((7,)),
    ]
    result = pl.pallas_call(
        kernel,
        out_shape=jax.ShapeDtypeStruct((TOK, COLS), BF),
        in_specs=[hbm, hbm, hbm, hbm, smem, smem, vmem],
        out_specs=vmem,
        scratch_shapes=scratch,
        compiler_params=pltpu.CompilerParams(
            collective_id=0, has_side_effects=True, vmem_limit_bytes=60 * 1024 * 1024
        ),
        name="spanned_attention",
    )(
        wide,
        states,
        neighbours.reshape(ROWS, COLS),
        cotangent,
        span_of,
        counts,
        gains.reshape(2, COLS),
    )
    return result.astype(F32)[None]


def solution(mesh):
    return jax.shard_map(
        per_device,
        mesh=mesh,
        in_specs=(
            P("dp", "mp"),
            P("dp", None, "mp"),
            P("dp", "mp"),
            P("dp"),
            P("dp"),
            P("group", "dp", None, "mp"),
            P("group", None, "mp"),
        ),
        out_specs=P("group", "dp", "mp"),
        check_vma=False,
    )
```
